256 devices in a mesh: mp: 8 (over z), dp: 32 (over y, x, core).
Axes of the slice: x: 4, y: 4, z: 8, core: 2. Of those that a mesh axis runs over, the one named last changes fastest.
Arguments:
- gate_partials: bfloat16 [32, 128, 73728], P('dp', 'mp'), as said below
- up_partials: bfloat16 [32, 128, 73728], P('dp', 'mp'), as said below
- gate_weight: float32 [128, 73728], P('mp', 'dp'), may hold values from -6 to 6
- up_weight: float32 [128, 73728], P('mp', 'dp'), may hold values from -6 to 6
- row_state: float32 [2, 128], P(None, 'mp'), may hold values from 0.1 to 10
- col_state: float32 [2, 73728], P(None, 'dp'), may hold values from 0.1 to 10
Outputs:
- new_gate: float32 [128, 73728], P('mp', 'dp')
- new_up: float32 [128, 73728], P('mp', 'dp')
- new_rows: float32 [2, 128], P(None, 'mp')
- new_cols: float32 [2, 73728], P(None, 'dp')
The draws below stay inside these ranges and needn't reach their ends.
Inputs may be any that keep to these rules, and one draw needn't show every extreme that they name: `gate_partials`: partial gradients of one weight slab; entries are finite. `up_partials`: partial gradients of one weight slab; entries are finite.
All inputs are finite; a program needn't handle non-finite values.
Results may differ from the reference program's by a relative error of at most 0.0003.
Values sent between devices are 32-bit elements; how exact they have to be, the bound alone decides.
A program may use at most 64 MiB of HBM per device.

```python
import math
import jax
import jax.numpy as jnp
from jax import lax

FF = 73728
ROWS = 128
NDP = 32


def scaled(base_key, noise, common):
    row_key, col_key, perm_key = jax.random.split(base_key, 3)
    row_place = jnp.arange(ROWS, dtype=jnp.float32) / ROWS
    col_place = jnp.arange(FF, dtype=jnp.float32) / FF
    row_scale = jnp.exp(math.log(3.0) * row_place + math.log(4.0) * jax.random.uniform(row_key, (ROWS,)))
    col_scale = jnp.exp(math.log(3.0) * col_place + math.log(4.0) * jax.random.uniform(col_key, (FF,)))
    order = jax.random.permutation(perm_key, NDP)
    block_index = jnp.arange(FF, dtype=jnp.int32) // (FF // NDP)
    boosted = jnp.where(order[:, None] == block_index[None, :], 3.0, 1.0)
    values = (noise + common) * row_scale[None, :, None] * col_scale[None, None, :]
    return values * boosted[:, None, :] / (4.0 * math.sqrt(NDP))


def partial_law(base_key, shrink):
    noise_key, common_key, scale_key = jax.random.split(base_key, 3)
    noise = jax.random.normal(noise_key, (NDP, ROWS, FF), jnp.float32)
    common = 0.3 * jax.random.normal(common_key, (1, ROWS, FF), jnp.float32)
    return (shrink * scaled(scale_key, noise, common)).astype(jnp.bfloat16)


def draw_gate_partials(key, part):
    key = jax.random.fold_in(key, 11)
    shrink = 0.006
    return partial_law(key, shrink)


def draw_up_partials(key, part):
    key = jax.random.fold_in(key, 23)
    shrink = 1.0
    return partial_law(key, shrink)


def level_of(rng, extent, cuts, low, top_value):
    gain, own = 1.0, jax.random.fold_in(rng, 6)
    for dim, parts in cuts:
        draws = jnp.exp(jax.random.uniform(jax.random.fold_in(own, dim), (parts,), jnp.float32, low / len(cuts), top_value / len(cuts)))
        gain = gain * jnp.repeat(draws, extent[dim] // parts).reshape([-1 if axis == dim else 1 for axis in range(len(extent))])
    return gain


def normal_values(own_key, dims, deviation, bound, cuts=(), kind=jnp.bfloat16):
    gain = level_of(own_key, dims, cuts, -0.22, 0.18) if cuts else 1.0
    result = jax.random.normal(own_key, dims, jnp.float32) * deviation * gain
    return jnp.minimum(jnp.maximum(result, -bound), bound).astype(kind)


def setup_inputs(seed: int = 0) -> dict:
    keys = jax.random.split(jax.random.key(seed), 7)
    gate_partials = draw_gate_partials(jax.random.fold_in(keys[6], 71), 0)
    up_partials = draw_up_partials(jax.random.fold_in(keys[6], 71), 0)
    gate_weight = normal_values(keys[2], (ROWS, FF), 1.0, 6.0, ((0, 8), (1, 32)), jnp.float32)
    up_weight = normal_values(keys[3], (ROWS, FF), 1.0, 6.0, ((0, 8), (1, 32)), jnp.float32)
    row_state = jnp.clip(jnp.exp(math.log(10.0) - 4.6051702 * jax.random.uniform(keys[4], (2, ROWS), jnp.float32) ** level_of(keys[4], (2, ROWS), ((1, 8),), -0.2, 0.2)), 0.1, 10.0)
    col_state = jnp.clip(jnp.exp(math.log(10.0) - 4.6051702 * jax.random.uniform(keys[5], (2, FF), jnp.float32) ** level_of(keys[5], (2, FF), ((1, 32),), -0.2, 0.2)), 0.1, 10.0)
    return {"gate_partials": gate_partials, "up_partials": up_partials, "gate_weight": gate_weight, "up_weight": up_weight, "row_state": row_state, "col_state": col_state}


second_decay = 0.8
clip_limit = 1.0
step_size = 0.5

def total_gradient(partials):
    start = jnp.zeros((ROWS, FF), jnp.float32)

    def add_one(index, carried):
        return carried + partials[index].astype(jnp.float32)
    return lax.fori_loop(0, NDP, add_one, start)

def reference(gate_partials, up_partials, gate_weight, up_weight, row_state, col_state):
    gradient = jnp.stack([total_gradient(gate_partials), total_gradient(up_partials)])
    squares = gradient * gradient
    row_sums = lax.optimization_barrier(jnp.sum(squares, axis=2))
    col_sums = lax.optimization_barrier(jnp.sum(squares, axis=1))
    new_rows = second_decay * row_state + (1.0 - second_decay) * row_sums / FF
    new_cols = second_decay * col_state + (1.0 - second_decay) * col_sums / ROWS
    row_mean = lax.optimization_barrier(jnp.sum(new_rows, axis=1)) / ROWS
    second = new_rows[:, :, None] * new_cols[:, None, :] / row_mean[:, None, None]
    update = gradient / jnp.sqrt(second)
    rms_value = jnp.sqrt(lax.optimization_barrier(jnp.sum(update * update, axis=(1, 2))) / (ROWS * FF))
    factor = 1.0 / jnp.maximum(1.0, rms_value / clip_limit)
    new_gate = gate_weight - step_size * factor[0] * update[0]
    new_up = up_weight - step_size * factor[1] * update[1]
    return (new_gate, new_up, new_rows, new_cols)
```

```python
import functools

import jax
import jax.numpy as jnp
from jax import lax
from jax.experimental import pallas as pl
from jax.experimental.pallas import tpu as pltpu
from jax.sharding import PartitionSpec as P

ROWS = 128
FF = 73728
DECAY = 0.8
STEP = 0.5
NZ, NY, NX, NC = 8, 4, 4, 2
NDP = NY * NX * NC
BLOCK = FF // NDP
HALF = 8
LANE = 128
WIDE = 3 * LANE
CHUNKS = tuple((m, j * 2 * WIDE, WIDE) for m in range(2) for j in range(BLOCK // (2 * WIDE)))
K = len(CHUNKS)
MESH = pl.DeviceIdType.MESH


def kernel(
    gate_hbm, up_hbm, gate_w_hbm, up_w_hbm, rows_hbm, cols_hbm,
    new_gate_hbm, new_up_hbm, new_rows_hbm, new_cols_hbm,
    inb, give, work, far, acc, direct, far2, acc2, direct2, grad,
    weight, row_state, col_state, new_rows, new_cols, col_all, row_all, sum_all, result,
    in_sem, core_send, core_recv, s1_send, s1_recv, s2_send, s2_recv,
    col_send, col_recv, row_send, row_recv, sum_send, sum_recv, w_sem, out_sem,
):
    z = lax.axis_index("mp")
    d = lax.axis_index("dp")
    y, x, c = d // (NX * NC), (d // NC) % NX, d % NC

    def device(zz, yy, xx, cc):
        return (lax.rem(zz, NZ), (lax.rem(yy, NY) * NX + lax.rem(xx, NX)) * NC + lax.rem(cc, NC))

    sibling = device(z, y, x, c + 1)
    step_x = (device(z, y, x + 1, c), device(z, y, x + NX - 1, c))
    step_y = (device(z, y + 1, x, c), device(z, y + NY - 1, x, c))
    plane = [
        device(z, y + dy, x + dx, c + dc)
        for dy in (2, 1, 3, 0) for dx in (2, 1, 3, 0) for dc in (1, 0) if (dy, dx, dc) != (0, 0, 0)
    ]
    column = [device(z + k, y, x, c) for k in (4, 3, 5, 2, 6, 1, 7)]

    barrier = pltpu.get_barrier_semaphore()
    for peer in column + plane:
        pl.semaphore_signal(barrier, 1, device_id=peer, device_id_type=MESH)

    partials = (gate_hbm, up_hbm)

    def load(k):
        m, first, wide = CHUNKS[k]

        def one(i, carry):
            ry, rx = i // NX, i % NX
            owner = (lax.rem(y + ry, NY) * NX + lax.rem(x + rx, NX)) * NC
            for side in range(2):
                core = (1 - c) if side == 0 else c
                start = pl.multiple_of((owner + core) * BLOCK + first, LANE)
                pltpu.make_async_copy(
                    partials[m].at[0, :, pl.ds(start, 2 * wide)], inb.at[k, side, ry, rx], in_sem.at[k, side]
                ).start()
            return carry

        lax.fori_loop(0, NY * NX, one, 0)

    for k in range(K):
        load(k)
    pltpu.make_async_copy(gate_w_hbm, weight.at[0], w_sem.at[0]).start()
    pltpu.make_async_copy(up_w_hbm, weight.at[1], w_sem.at[1]).start()
    pltpu.make_async_copy(rows_hbm, row_state, w_sem.at[2]).start()
    pltpu.make_async_copy(cols_hbm, col_state, w_sem.at[3]).start()

    def wait_load(k, side):
        pltpu.make_async_copy(inb.at[k, side], inb.at[k, side], in_sem.at[k, side]).wait()

    started = []

    def send(src, dst, send_sem, recv_sem, target):
        copy = pltpu.make_async_remote_copy(
            src_ref=src, dst_ref=dst, send_sem=send_sem, recv_sem=recv_sem, device_id=target, device_id_type=MESH
        )
        copy.start()
        started.append(copy)
        return copy

    def convert(k):
        wait_load(k, 0)
        wide = CHUNKS[k][2]

        def one(i, carry):
            ry, rx = i // NX, i % NX
            value = inb[k, 0, ry, rx].astype(jnp.float32)
            for h in range(2):
                part = value[:, h * wide : (h + 1) * wide]
                give[k, 0, h, rx, ry] = part[:HALF]
                give[k, 1, h, ry, rx] = part[HALF:]
            return carry

        lax.fori_loop(0, NY * NX, one, 0)

    def exchange(k):
        return send(give.at[k], work.at[k], core_send.at[k], core_recv.at[k], sibling)

    def add_own(k):
        wait_load(k, 1)
        wide = CHUNKS[k][2]

        def one(i, carry):
            ry, rx = i // NX, i % NX
            value = inb[k, 1, ry, rx].astype(jnp.float32)
            for h in range(2):
                part = value[:, h * wide : (h + 1) * wide]
                work[k, 0, h, rx, ry] = work[k, 0, h, rx, ry] + part[:HALF]
                work[k, 1, h, ry, rx] = work[k, 1, h, ry, rx] + part[HALF:]
            return carry

        lax.fori_loop(0, NY * NX, one, 0)

    near = (1, 3)
    pairs = [(p, h) for h in range(2) for p in range(2)]
    copies = {}

    def first_sends(k):
        for p, h in pairs:
            step = (step_x, step_y)[p]
            copies[k, p, h, "far"] = send(
                work.at[k, p, h, 2], far.at[k, p, h], s1_send.at[k, p, h, 0], s1_recv.at[k, p, h, 0], step[h])
        for p, h in pairs:
            step = (step_x, step_y)[p]
            copies[k, p, h, "direct"] = send(
                work.at[k, p, h, near[1 - h]], direct.at[k, p, h], s1_send.at[k, p, h, 1], s1_recv.at[k, p, h, 1],
                step[1 - h])

    def first_join(k):
        for p, h in pairs:
            step = (step_x, step_y)[p]
            copies[k, p, h, "far"].wait_recv()
            work[k, p, h, near[h]] = work[k, p, h, near[h]] + far[k, p, h]
            copies[k, p, h, "acc"] = send(
                work.at[k, p, h, near[h]], acc.at[k, p, h], s1_send.at[k, p, h, 2], s1_recv.at[k, p, h, 2], step[h])

    def second_sends(k):
        for p, h in pairs:
            step = (step_y, step_x)[p]
            copies[k, p, h, "direct"].wait_recv()
            copies[k, p, h, "acc"].wait_recv()
            work[k, p, h, 0] = work[k, p, h, 0] + direct[k, p, h] + acc[k, p, h]
            copies[k, p, h, "far2"] = send(
                work.at[k, p, h, 0, 2], far2.at[k, p, h], s2_send.at[k, p, h, 0], s2_recv.at[k, p, h, 0], step[h])
            copies[k, p, h, "direct2"] = send(
                work.at[k, p, h, 0, near[1 - h]], direct2.at[k, p, h], s2_send.at[k, p, h, 1],
                s2_recv.at[k, p, h, 1], step[1 - h])

    def second_join(k):
        for p, h in pairs:
            step = (step_y, step_x)[p]
            copies[k, p, h, "far2"].wait_recv()
            work[k, p, h, 0, near[h]] = work[k, p, h, 0, near[h]] + far2[k, p, h]
            copies[k, p, h, "acc2"] = send(
                work.at[k, p, h, 0, near[h]], acc2.at[k, p, h], s2_send.at[k, p, h, 2], s2_recv.at[k, p, h, 2],
                step[h])

    lane_sums = [None, None]

    def lanes(value):
        total = value[:, :LANE]
        for j in range(1, value.shape[1] // LANE):
            total = total + value[:, j * LANE : (j + 1) * LANE]
        return total

    def finish(k):
        m, first, wide = CHUNKS[k]
        for p, h in pairs:
            copies[k, p, h, "direct2"].wait_recv()
            copies[k, p, h, "acc2"].wait_recv()
            grad[m, p * HALF : (p + 1) * HALF, first + h * wide : first + (h + 1) * wide] = (
                work[k, p, h, 0, 0] + direct2[k, p, h] + acc2[k, p, h])
        g = grad[m, :, first : first + 2 * wide]
        squares = g * g
        col_all[k, z] = jnp.sum(squares, axis=0, keepdims=True)
        for i, peer in enumerate(column):
            send(col_all.at[k, z], col_all.at[k, z], col_send.at[k, i], col_recv.at[k, i], peer)
        part = lanes(squares)
        lane_sums[m] = part if lane_sums[m] is None else lane_sums[m] + part

    def wait_columns(k):
        for i in range(NZ - 1):
            source = lax.rem(z + NZ - (4, 3, 5, 2, 6, 1, 7)[i], NZ)
            pltpu.make_async_remote_copy(
                src_ref=col_all.at[k, source], dst_ref=col_all.at[k, source], send_sem=col_send.at[k, i],
                recv_sem=col_recv.at[k, i], device_id=sibling, device_id_type=MESH).wait_recv()

    for k in range(K):
        convert(k)
        if k == 0:
            pl.semaphore_wait(barrier, len(plane) + len(column))
        copies[k, "core"] = exchange(k)
        if k > 0:
            copies[k - 1, "core"].wait_recv()
            add_own(k - 1)
            first_sends(k - 1)
    copies[K - 1, "core"].wait_recv()
    add_own(K - 1)
    first_sends(K - 1)
    for k in range(K):
        first_join(k)
    for k in range(K):
        second_sends(k)
    for k in range(K):
        second_join(k)
    for k in range(K):
        finish(k)

    row_id = lax.broadcasted_iota(jnp.int32, (16, LANE), 0)
    lane_id = lax.broadcasted_iota(jnp.int32, (16, LANE), 1)
    lane_one = lax.broadcasted_iota(jnp.int32, (1, LANE), 1)
    small_row = lax.broadcasted_iota(jnp.int32, (16, 16), 0)
    small_lane = lax.broadcasted_iota(jnp.int32, (16, 16), 1)

    row_sums = [jnp.sum(lane_sums[m], axis=1, keepdims=True) for m in range(2)]
    for i in range(4):
        ref = (weight.at[0], weight.at[1], row_state, col_state)[i]
        pltpu.make_async_copy(ref, ref, w_sem.at[i]).wait()
    old_rows = [
        jnp.sum(jnp.where(small_row == small_lane, row_state[m : m + 1, :], 0.0), axis=1, keepdims=True)
        for m in range(2)
    ]

    scaled = [None, None]
    for k in range(K):
        m, first, wide = CHUNKS[k]
        wait_columns(k)
        total = col_all[k, 0]
        for j in range(1, NZ):
            total = total + col_all[k, j]
        span = slice(first, first + 2 * wide)
        fresh = DECAY * col_state[m : m + 1, span] + (1.0 - DECAY) * total / ROWS
        new_cols[m : m + 1, span] = fresh
        g = grad[m, :, span]
        part = lanes(g * g * (1.0 / fresh))
        scaled[m] = part if scaled[m] is None else scaled[m] + part
    scaled = [jnp.sum(scaled[m], axis=1, keepdims=True) for m in range(2)]

    packed = jnp.zeros((16, LANE), jnp.float32)
    for q, value in enumerate(row_sums + scaled):
        packed = jnp.where(lane_id == row_id + 16 * q, value, packed)
    row_all[d] = jnp.sum(packed, axis=0, keepdims=True)
    for i, peer in enumerate(plane):
        send(row_all.at[d], row_all.at[d], row_send.at[i], row_recv.at[i], peer)

    out_cols = pltpu.make_async_copy(new_cols, new_cols_hbm, out_sem.at[0])
    out_cols.start()
    for m in range(2):
        grad[m] = grad[m] * lax.rsqrt(new_cols[m : m + 1, :])

    offsets = [
        (dy, dx, dc) for dy in (2, 1, 3, 0) for dx in (2, 1, 3, 0) for dc in (1, 0) if (dy, dx, dc) != (0, 0, 0)
    ]
    for i, (dy, dx, dc) in enumerate(offsets):
        source = device(z, y + NY - dy, x + NX - dx, c + dc)[1]
        pltpu.make_async_remote_copy(
            src_ref=row_all.at[source], dst_ref=row_all.at[source], send_sem=row_send.at[i],
            recv_sem=row_recv.at[i], device_id=sibling, device_id_type=MESH).wait_recv()
    total = row_all[0]
    for j in range(1, NDP):
        total = total + row_all[j]
    spread = jnp.broadcast_to(total, (16, LANE))
    part = [
        jnp.sum(jnp.where(lane_id == row_id + 16 * q, spread, 0.0), axis=1, keepdims=True) for q in range(4)
    ]
    fresh_rows = [DECAY * old_rows[m] + (1.0 - DECAY) * part[m] / FF for m in range(2)]
    message = jnp.zeros((1, LANE), jnp.float32)
    for m in range(2):
        message = jnp.where(lane_one == m, jnp.sum(part[2 + m] / fresh_rows[m], axis=0, keepdims=True), message)
        message = jnp.where(lane_one == 2 + m, jnp.sum(fresh_rows[m], axis=0, keepdims=True), message)
    sum_all[z] = message
    for i, peer in enumerate(column):
        send(sum_all.at[z], sum_all.at[z], sum_send.at[i], sum_recv.at[i], peer)

    for m in range(2):
        new_rows[m : m + 1, :] = jnp.sum(
            jnp.where(small_row == small_lane, fresh_rows[m], 0.0), axis=0, keepdims=True)
        grad[m] = grad[m] * lax.rsqrt(fresh_rows[m])
    out_rows = pltpu.make_async_copy(new_rows, new_rows_hbm, out_sem.at[1])
    out_rows.start()

    for i in range(NZ - 1):
        source = lax.rem(z + NZ - (4, 3, 5, 2, 6, 1, 7)[i], NZ)
        pltpu.make_async_remote_copy(
            src_ref=sum_all.at[source], dst_ref=sum_all.at[source], send_sem=sum_send.at[i],
            recv_sem=sum_recv.at[i], device_id=sibling, device_id_type=MESH).wait_recv()
    total = sum_all[0]
    for j in range(1, NZ):
        total = total + sum_all[j]
    outs = []
    for m in range(2):
        squares = jnp.sum(jnp.where(lane_one == m, total, 0.0), axis=1, keepdims=True)
        mean = jnp.sum(jnp.where(lane_one == 2 + m, total, 0.0), axis=1, keepdims=True) / ROWS
        root = jnp.sqrt(mean)
        rms = root * jnp.sqrt(squares / (ROWS * FF))
        scale = STEP * root / jnp.maximum(1.0, rms)
        result[m] = weight[m] - grad[m] * scale
        out = pltpu.make_async_copy(result.at[m], (new_gate_hbm, new_up_hbm)[m], out_sem.at[2 + m])
        out.start()
        outs.append(out)
    for copy in started:
        copy.wait_send()
    out_cols.wait()
    out_rows.wait()
    for out in outs:
        out.wait()


def on_device(gate_partials, up_partials, gate_weight, up_weight, row_state, col_state):
    f32 = jnp.float32
    dma = pltpu.SemaphoreType.DMA
    return pl.pallas_call(
        kernel,
        out_shape=(
            jax.ShapeDtypeStruct((16, BLOCK), f32),
            jax.ShapeDtypeStruct((16, BLOCK), f32),
            jax.ShapeDtypeStruct((2, 16), f32),
            jax.ShapeDtypeStruct((2, BLOCK), f32),
        ),
        in_specs=[pl.BlockSpec(memory_space=pl.ANY)] * 6,
        out_specs=(pl.BlockSpec(memory_space=pl.ANY),) * 4,
        scratch_shapes=[
            pltpu.VMEM((K, 2, NY, NX, 16, 2 * WIDE), jnp.bfloat16),
            pltpu.VMEM((K, 2, 2, 4, 4, HALF, WIDE), f32),
            pltpu.VMEM((K, 2, 2, 4, 4, HALF, WIDE), f32),
            pltpu.VMEM((K, 2, 2, 4, HALF, WIDE), f32),
            pltpu.VMEM((K, 2, 2, 4, HALF, WIDE), f32),
            pltpu.VMEM((K, 2, 2, 4, HALF, WIDE), f32),
            pltpu.VMEM((K, 2, 2, HALF, WIDE), f32),
            pltpu.VMEM((K, 2, 2, HALF, WIDE), f32),
            pltpu.VMEM((K, 2, 2, HALF, WIDE), f32),
            pltpu.VMEM((2, 16, BLOCK), f32),
            pltpu.VMEM((2, 16, BLOCK), f32),
            pltpu.VMEM((2, 16), f32),
            pltpu.VMEM((2, BLOCK), f32),
            pltpu.VMEM((2, 16), f32),
            pltpu.VMEM((2, BLOCK), f32),
            pltpu.VMEM((K, NZ, 1, 2 * WIDE), f32),
            pltpu.VMEM((NDP, 1, LANE), f32),
            pltpu.VMEM((NZ, 1, LANE), f32),
            pltpu.VMEM((2, 16, BLOCK), f32),
            dma((K, 2)),
            dma((K,)),
            dma((K,)),
            dma((K, 2, 2, 3)),
            dma((K, 2, 2, 3)),
            dma((K, 2, 2, 3)),
            dma((K, 2, 2, 3)),
            dma((K, NZ - 1)),
            dma((K, NZ - 1)),
            dma((NDP - 1,)),
            dma((NDP - 1,)),
            dma((NZ - 1,)),
            dma((NZ - 1,)),
            dma((4,)),
            dma((4,)),
        ],
        compiler_params=pltpu.CompilerParams(
            collective_id=0, has_side_effects=True, vmem_limit_bytes=48 * 1024 * 1024
        ),
    )(gate_partials, up_partials, gate_weight, up_weight, row_state, col_state)


def solution(mesh):
    placed = (
        P("dp", "mp", None),
        P("dp", "mp", None),
        P("mp", "dp"),
        P("mp", "dp"),
        P(None, "mp"),
        P(None, "dp"),
    )
    return jax.shard_map(
        on_device,
        mesh=mesh,
        in_specs=placed,
        out_specs=(P("mp", "dp"), P("mp", "dp"), P(None, "mp"), P(None, "dp")),
        check_vma=False,
    )
```

```python
import functools

import jax
import jax.numpy as jnp
from jax import lax
from jax.experimental import pallas as pl
from jax.experimental.pallas import tpu as pltpu
from jax.sharding import PartitionSpec as P

ROWS = 128
FF = 73728
DECAY = 0.8
STEP = 0.5
NZ, NY, NX, NC = 8, 4, 4, 2
NDP = NY * NX * NC
BLOCK = FF // NDP
HALF = 8
LANE = 128
WIDE = 3 * LANE
CHUNKS = tuple((m, j * 2 * WIDE, WIDE) for m in range(2) for j in range(BLOCK // (2 * WIDE)))
K = len(CHUNKS)
MESH = pl.DeviceIdType.MESH


def kernel(
    gate_hbm, up_hbm, rows_hbm, cols_hbm,
    shape_hbm, sums_hbm, new_rows_hbm, new_cols_hbm,
    inb, give, work, far, acc, direct, far2, acc2, direct2, grad,
    row_state, col_state, new_rows, new_cols, col_all, row_all, sum_all, sums,
    in_sem, core_send, core_recv, s1_send, s1_recv, s2_send, s2_recv,
    col_send, col_recv, row_send, row_recv, sum_send, sum_recv, w_sem, out_sem,
):
    z = lax.axis_index("mp")
    d = lax.axis_index("dp")
    y, x, c = d // (NX * NC), (d // NC) % NX, d % NC

    def device(zz, yy, xx, cc):
        return (lax.rem(zz, NZ), (lax.rem(yy, NY) * NX + lax.rem(xx, NX)) * NC + lax.rem(cc, NC))

    sibling = device(z, y, x, c + 1)
    step_x = (device(z, y, x + 1, c), device(z, y, x + NX - 1, c))
    step_y = (device(z, y + 1, x, c), device(z, y + NY - 1, x, c))
    plane = [
        device(z, y + dy, x + dx, c + dc)
        for dy in (2, 1, 3, 0) for dx in (2, 1, 3, 0) for dc in (1, 0) if (dy, dx, dc) != (0, 0, 0)
    ]
    column = [device(z + k, y, x, c) for k in (4, 3, 5, 2, 6, 1, 7)]

    partials = (gate_hbm, up_hbm)

    loads = [pltpu.make_async_copy(partials[m].at[0], inb.at[m], in_sem.at[m]) for m in range(2)]
    for copy in loads:
        copy.start()
    barrier = pltpu.get_barrier_semaphore()
    greeted = [*step_x, *step_y, sibling, *column]
    for peer in greeted:
        pl.semaphore_signal(barrier, 1, device_id=peer, device_id_type=MESH)
    pltpu.make_async_copy(rows_hbm, row_state, w_sem.at[0]).start()
    pltpu.make_async_copy(cols_hbm, col_state, w_sem.at[1]).start()

    def own_block(k, i, core):
        m, first, wide = CHUNKS[k]
        owner = (lax.rem(y + i // NX, NY) * NX + lax.rem(x + i % NX, NX)) * NC + core
        start = pl.multiple_of(owner * BLOCK + first, LANE)
        return inb[m, :, pl.ds(start, 2 * wide)].astype(jnp.float32)

    started = []

    def send(src, dst, send_sem, recv_sem, target):
        copy = pltpu.make_async_remote_copy(
            src_ref=src, dst_ref=dst, send_sem=send_sem, recv_sem=recv_sem, device_id=target, device_id_type=MESH
        )
        copy.start()
        started.append(copy)
        return copy

    def convert(k):
        wide = CHUNKS[k][2]

        def one(i, carry):
            ry, rx = i // NX, i % NX
            value = own_block(k, i, 1 - c)
            for h in range(2):
                part = value[:, h * wide : (h + 1) * wide]
                give[k, 0, h, rx, ry] = part[:HALF]
                give[k, 1, h, ry, rx] = part[HALF:]
            return carry

        lax.fori_loop(0, NY * NX, one, 0, unroll=4)

    def exchange(k):
        return send(give.at[k], work.at[k], core_send.at[k], core_recv.at[k], sibling)

    def add_own(k):
        wide = CHUNKS[k][2]

        def one(i, carry):
            ry, rx = i // NX, i % NX
            value = own_block(k, i, c)
            for h in range(2):
                part = value[:, h * wide : (h + 1) * wide]
                work[k, 0, h, rx, ry] = work[k, 0, h, rx, ry] + part[:HALF]
                work[k, 1, h, ry, rx] = work[k, 1, h, ry, rx] + part[HALF:]
            return carry

        lax.fori_loop(0, NY * NX, one, 0, unroll=4)

    near = (1, 3)
    pairs = [(p, h) for h in range(2) for p in range(2)]
    copies = {}

    def first_sends(k):
        for p, h in pairs:
            step = (step_x, step_y)[p]
            copies[k, p, h, "far"] = send(
                work.at[k, p, h, 2], far.at[k, p, h], s1_send.at[k, p, h, 0], s1_recv.at[k, p, h, 0], step[h])
        for p, h in pairs:
            step = (step_x, step_y)[p]
            copies[k, p, h, "direct"] = send(
                work.at[k, p, h, near[1 - h]], direct.at[k, p, h], s1_send.at[k, p, h, 1], s1_recv.at[k, p, h, 1],
                step[1 - h])

    def first_join(k):
        for p, h in pairs:
            step = (step_x, step_y)[p]
            copies[k, p, h, "far"].wait_recv()
            work[k, p, h, near[h]] = work[k, p, h, near[h]] + far[k, p, h]
            copies[k, p, h, "acc"] = send(
                work.at[k, p, h, near[h]], acc.at[k, p, h], s1_send.at[k, p, h, 2], s1_recv.at[k, p, h, 2], step[h])

    def second_sends(k):
        for p, h in pairs:
            step = (step_y, step_x)[p]
            copies[k, p, h, "direct"].wait_recv()
            copies[k, p, h, "acc"].wait_recv()
            work[k, p, h, 0] = work[k, p, h, 0] + direct[k, p, h] + acc[k, p, h]
            copies[k, p, h, "far2"] = send(
                work.at[k, p, h, 0, 2], far2.at[k, p, h], s2_send.at[k, p, h, 0], s2_recv.at[k, p, h, 0], step[h])
            copies[k, p, h, "direct2"] = send(
                work.at[k, p, h, 0, near[1 - h]], direct2.at[k, p, h], s2_send.at[k, p, h, 1],
                s2_recv.at[k, p, h, 1], step[1 - h])

    def second_join(k):
        for p, h in pairs:
            step = (step_y, step_x)[p]
            copies[k, p, h, "far2"].wait_recv()
            work[k, p, h, 0, near[h]] = work[k, p, h, 0, near[h]] + far2[k, p, h]
            copies[k, p, h, "acc2"] = send(
                work.at[k, p, h, 0, near[h]], acc2.at[k, p, h], s2_send.at[k, p, h, 2], s2_recv.at[k, p, h, 2],
                step[h])

    lane_sums = [None, None]

    def lanes(value):
        total = value[:, :LANE]
        for j in range(1, value.shape[1] // LANE):
            total = total + value[:, j * LANE : (j + 1) * LANE]
        return total

    def finish(k):
        m, first, wide = CHUNKS[k]
        for p, h in pairs:
            copies[k, p, h, "direct2"].wait_recv()
            copies[k, p, h, "acc2"].wait_recv()
            grad[m, p * HALF : (p + 1) * HALF, first + h * wide : first + (h + 1) * wide] = (
                work[k, p, h, 0, 0] + direct2[k, p, h] + acc2[k, p, h])
        g = grad[m, :, first : first + 2 * wide]
        squares = g * g
        col_all[k, z] = jnp.sum(squares, axis=0, keepdims=True)
        for i, peer in enumerate(column):
            send(col_all.at[k, z], col_all.at[k, z], col_send.at[k, i], col_recv.at[k, i], peer)
        part = lanes(squares)
        lane_sums[m] = part if lane_sums[m] is None else lane_sums[m] + part

    def wait_columns(k):
        for i in range(NZ - 1):
            source = lax.rem(z + NZ - (4, 3, 5, 2, 6, 1, 7)[i], NZ)
            pltpu.make_async_remote_copy(
                src_ref=col_all.at[k, source], dst_ref=col_all.at[k, source], send_sem=col_send.at[k, i],
                recv_sem=col_recv.at[k, i], device_id=sibling, device_id_type=MESH).wait_recv()

    for k in range(K):
        if k == 0 or CHUNKS[k][0] != CHUNKS[k - 1][0]:
            loads[CHUNKS[k][0]].wait()
        convert(k)
        if k == 0:
            pl.semaphore_wait(barrier, len(greeted))
        copies[k, "core"] = exchange(k)
        if k > 0:
            copies[k - 1, "core"].wait_recv()
            add_own(k - 1)
            first_sends(k - 1)
    copies[K - 1, "core"].wait_recv()
    add_own(K - 1)
    first_sends(K - 1)
    for k in range(K):
        first_join(k)
    for k in range(K):
        second_sends(k)
    for k in range(K):
        second_join(k)
    for k in range(K):
        finish(k)

    row_id = lax.broadcasted_iota(jnp.int32, (16, LANE), 0)
    lane_id = lax.broadcasted_iota(jnp.int32, (16, LANE), 1)
    lane_one = lax.broadcasted_iota(jnp.int32, (1, LANE), 1)
    small_row = lax.broadcasted_iota(jnp.int32, (16, 16), 0)
    small_lane = lax.broadcasted_iota(jnp.int32, (16, 16), 1)

    row_sums = [jnp.sum(lane_sums[m], axis=1, keepdims=True) for m in range(2)]
    for i, ref in enumerate((row_state, col_state)):
        pltpu.make_async_copy(ref, ref, w_sem.at[i]).wait()
    old_rows = [
        jnp.sum(jnp.where(small_row == small_lane, row_state[m : m + 1, :], 0.0), axis=1, keepdims=True)
        for m in range(2)
    ]

    scaled = [None, None]
    for k in range(K):
        m, first, wide = CHUNKS[k]
        wait_columns(k)
        total = col_all[k, 0]
        for j in range(1, NZ):
            total = total + col_all[k, j]
        span = slice(first, first + 2 * wide)
        fresh = DECAY * col_state[m : m + 1, span] + (1.0 - DECAY) * total / ROWS
        new_cols[m : m + 1, span] = fresh
        g = grad[m, :, span]
        part = lanes(g * g * (1.0 / fresh))
        scaled[m] = part if scaled[m] is None else scaled[m] + part
    scaled = [jnp.sum(scaled[m], axis=1, keepdims=True) for m in range(2)]

    packed = jnp.zeros((16, LANE), jnp.float32)
    for q, value in enumerate(row_sums + scaled):
        packed = jnp.where(lane_id == row_id + 16 * q, value, packed)
    row_all[d] = jnp.sum(packed, axis=0, keepdims=True)
    for i, peer in enumerate(plane):
        send(row_all.at[d], row_all.at[d], row_send.at[i], row_recv.at[i], peer)

    out_cols = pltpu.make_async_copy(new_cols, new_cols_hbm, out_sem.at[0])
    out_cols.start()
    for m in range(2):
        grad[m] = grad[m] * lax.rsqrt(new_cols[m : m + 1, :])

    offsets = [
        (dy, dx, dc) for dy in (2, 1, 3, 0) for dx in (2, 1, 3, 0) for dc in (1, 0) if (dy, dx, dc) != (0, 0, 0)
    ]
    for i, (dy, dx, dc) in enumerate(offsets):
        source = device(z, y + NY - dy, x + NX - dx, c + dc)[1]
        pltpu.make_async_remote_copy(
            src_ref=row_all.at[source], dst_ref=row_all.at[source], send_sem=row_send.at[i],
            recv_sem=row_recv.at[i], device_id=sibling, device_id_type=MESH).wait_recv()
    total = row_all[0]
    for j in range(1, NDP):
        total = total + row_all[j]
    spread = jnp.broadcast_to(total, (16, LANE))
    part = [
        jnp.sum(jnp.where(lane_id == row_id + 16 * q, spread, 0.0), axis=1, keepdims=True) for q in range(4)
    ]
    fresh_rows = [DECAY * old_rows[m] + (1.0 - DECAY) * part[m] / FF for m in range(2)]
    message = jnp.zeros((1, LANE), jnp.float32)
    for m in range(2):
        message = jnp.where(lane_one == m, jnp.sum(part[2 + m] / fresh_rows[m], axis=0, keepdims=True), message)
        message = jnp.where(lane_one == 2 + m, jnp.sum(fresh_rows[m], axis=0, keepdims=True), message)
    sum_all[z] = message
    for i, peer in enumerate(column):
        send(sum_all.at[z], sum_all.at[z], sum_send.at[i], sum_recv.at[i], peer)

    for m in range(2):
        new_rows[m : m + 1, :] = jnp.sum(
            jnp.where(small_row == small_lane, fresh_rows[m], 0.0), axis=0, keepdims=True)
        grad[m] = grad[m] * lax.rsqrt(fresh_rows[m])
    out_rows = pltpu.make_async_copy(new_rows, new_rows_hbm, out_sem.at[1])
    out_rows.start()
    out_shape = pltpu.make_async_copy(grad, shape_hbm, out_sem.at[2])
    out_shape.start()
    for copy in started[:-len(column)]:
        copy.wait_send()

    for i in range(NZ - 1):
        source = lax.rem(z + NZ - (4, 3, 5, 2, 6, 1, 7)[i], NZ)
        pltpu.make_async_remote_copy(
            src_ref=sum_all.at[source], dst_ref=sum_all.at[source], send_sem=sum_send.at[i],
            recv_sem=sum_recv.at[i], device_id=sibling, device_id_type=MESH).wait_recv()
    total = sum_all[0]
    for j in range(1, NZ):
        total = total + sum_all[j]
    sums[...] = total
    out_sums = pltpu.make_async_copy(sums, sums_hbm, out_sem.at[3])
    out_sums.start()
    for copy in started[-len(column):]:
        copy.wait_send()
    for out in (out_cols, out_rows, out_shape, out_sums):
        out.wait()


def apply(
    shape_hbm, sums_hbm, rows_hbm, cols_hbm, gate_w_hbm, up_w_hbm,
    new_gate_hbm, new_up_hbm, new_rows_hbm, new_cols_hbm,
    shape, sums, weight, in_sem, out_sem,
):
    loads = [
        pltpu.make_async_copy(src, dst, in_sem.at[i])
        for i, (src, dst) in enumerate((
            (sums_hbm, sums), (shape_hbm.at[0], shape.at[0]), (gate_w_hbm, weight.at[0]),
            (shape_hbm.at[1], shape.at[1]), (up_w_hbm, weight.at[1])))
    ]
    outs = [
        pltpu.make_async_copy(rows_hbm, new_rows_hbm, out_sem.at[2]),
        pltpu.make_async_copy(cols_hbm, new_cols_hbm, out_sem.at[3]),
    ]
    for copy in loads + outs:
        copy.start()
    loads[0].wait()
    lane = lax.broadcasted_iota(jnp.int32, (1, LANE), 1)
    total = sums[...]
    scales = []
    for m in range(2):
        squares = jnp.sum(jnp.where(lane == m, total, 0.0), axis=1, keepdims=True)
        mean = jnp.sum(jnp.where(lane == 2 + m, total, 0.0), axis=1, keepdims=True) / ROWS
        root = jnp.sqrt(mean)
        rms = root * jnp.sqrt(squares / (ROWS * FF))
        scales.append(STEP * root / jnp.maximum(1.0, rms))
    for m in range(2):
        loads[1 + 2 * m].wait()
        loads[2 + 2 * m].wait()
        weight[m] = weight[m] - shape[m] * scales[m]
        out = pltpu.make_async_copy(weight.at[m], (new_gate_hbm, new_up_hbm)[m], out_sem.at[m])
        out.start()
        outs.append(out)
    for out in outs:
        out.wait()


def on_device(gate_partials, up_partials, gate_weight, up_weight, row_state, col_state):
    f32 = jnp.float32
    dma = pltpu.SemaphoreType.DMA
    shape, sums, new_rows, new_cols = pl.pallas_call(
        kernel,
        out_shape=(
            jax.ShapeDtypeStruct((2, 16, BLOCK), f32),
            jax.ShapeDtypeStruct((1, LANE), f32),
            jax.ShapeDtypeStruct((2, 16), f32),
            jax.ShapeDtypeStruct((2, BLOCK), f32),
        ),
        in_specs=[pl.BlockSpec(memory_space=pl.ANY)] * 4,
        out_specs=(pl.BlockSpec(memory_space=pl.ANY),) * 4,
        scratch_shapes=[
            pltpu.VMEM((2, 16, FF), jnp.bfloat16),
            pltpu.VMEM((K, 2, 2, 4, 4, HALF, WIDE), f32),
            pltpu.VMEM((K, 2, 2, 4, 4, HALF, WIDE), f32),
            pltpu.VMEM((K, 2, 2, 4, HALF, WIDE), f32),
            pltpu.VMEM((K, 2, 2, 4, HALF, WIDE), f32),
            pltpu.VMEM((K, 2, 2, 4, HALF, WIDE), f32),
            pltpu.VMEM((K, 2, 2, HALF, WIDE), f32),
            pltpu.VMEM((K, 2, 2, HALF, WIDE), f32),
            pltpu.VMEM((K, 2, 2, HALF, WIDE), f32),
            pltpu.VMEM((2, 16, BLOCK), f32),
            pltpu.VMEM((2, 16), f32),
            pltpu.VMEM((2, BLOCK), f32),
            pltpu.VMEM((2, 16), f32),
            pltpu.VMEM((2, BLOCK), f32),
            pltpu.VMEM((K, NZ, 1, 2 * WIDE), f32),
            pltpu.VMEM((NDP, 1, LANE), f32),
            pltpu.VMEM((NZ, 1, LANE), f32),
            pltpu.VMEM((1, LANE), f32),
            dma((2,)),
            dma((K,)),
            dma((K,)),
            dma((K, 2, 2, 3)),
            dma((K, 2, 2, 3)),
            dma((K, 2, 2, 3)),
            dma((K, 2, 2, 3)),
            dma((K, NZ - 1)),
            dma((K, NZ - 1)),
            dma((NDP - 1,)),
            dma((NDP - 1,)),
            dma((NZ - 1,)),
            dma((NZ - 1,)),
            dma((2,)),
            dma((4,)),
        ],
        compiler_params=pltpu.CompilerParams(
            collective_id=0, has_side_effects=True, vmem_limit_bytes=60 * 1024 * 1024
        ),
    )(gate_partials, up_partials, row_state, col_state)
    return pl.pallas_call(
        apply,
        out_shape=(
            jax.ShapeDtypeStruct((16, BLOCK), f32),
            jax.ShapeDtypeStruct((16, BLOCK), f32),
            jax.ShapeDtypeStruct((2, 16), f32),
            jax.ShapeDtypeStruct((2, BLOCK), f32),
        ),
        in_specs=[pl.BlockSpec(memory_space=pl.ANY)] * 6,
        out_specs=(pl.BlockSpec(memory_space=pl.ANY),) * 4,
        scratch_shapes=[
            pltpu.VMEM((2, 16, BLOCK), f32),
            pltpu.VMEM((1, LANE), f32),
            pltpu.VMEM((2, 16, BLOCK), f32),
            dma((5,)),
            dma((4,)),
        ],
        compiler_params=pltpu.CompilerParams(vmem_limit_bytes=60 * 1024 * 1024),
    )(shape, sums, new_rows, new_cols, gate_weight, up_weight)


def solution(mesh):
    placed = (
        P("dp", "mp", None),
        P("dp", "mp", None),
        P("mp", "dp"),
        P("mp", "dp"),
        P(None, "mp"),
        P(None, "dp"),
    )
    return jax.shard_map(
        on_device,
        mesh=mesh,
        in_specs=placed,
        out_specs=(P("mp", "dp"), P("mp", "dp"), P(None, "mp"), P(None, "dp")),
        check_vma=False,
    )
```

```python
import functools

import jax
import jax.numpy as jnp
from jax import lax
from jax.experimental import pallas as pl
from jax.experimental.pallas import tpu as pltpu
from jax.sharding import PartitionSpec as P

ROWS = 128
FF = 73728
DECAY = 0.8
STEP = 0.5
NZ, NY, NX, NC = 8, 4, 4, 2
NDP = NY * NX * NC
BLOCK = FF // NDP
HALF = 8
LANE = 128
TILES = ((3, 6), (6, 3))
CHUNKS = tuple(
    (m, 2 * LANE * sum(TILES[m][:j]), LANE * n) for m in range(2) for j, n in enumerate(TILES[m])
)
K = len(CHUNKS)
SHORT = 0
MESH = pl.DeviceIdType.MESH


def kernel(
    gate_hbm, up_hbm, rows_hbm, cols_hbm,
    shape_hbm, sums_hbm, new_rows_hbm, new_cols_hbm,
    inb, give, work, far, acc, direct, far2, acc2, direct2, grad,
    row_state, col_state, new_rows, new_cols, col_all, row_all, sum_all, sums,
    in_sem, core_send, core_recv, s1_send, s1_recv, s2_send, s2_recv,
    col_send, col_recv, row_send, row_recv, sum_send, sum_recv, w_sem, out_sem,
):
    z = lax.axis_index("mp")
    d = lax.axis_index("dp")
    y, x, c = d // (NX * NC), (d // NC) % NX, d % NC

    def device(zz, yy, xx, cc):
        return (lax.rem(zz, NZ), (lax.rem(yy, NY) * NX + lax.rem(xx, NX)) * NC + lax.rem(cc, NC))

    sibling = device(z, y, x, c + 1)
    step_x = (device(z, y, x + 1, c), device(z, y, x + NX - 1, c))
    step_y = (device(z, y + 1, x, c), device(z, y + NY - 1, x, c))
    plane = [
        device(z, y + dy, x + dx, c + dc)
        for dy in (2, 1, 3, 0) for dx in (2, 1, 3, 0) for dc in (1, 0) if (dy, dx, dc) != (0, 0, 0)
    ]
    column = [device(z + k, y, x, c) for k in (4, 3, 5, 2, 6, 1, 7)]

    partials = (gate_hbm, up_hbm)

    loads = [pltpu.make_async_copy(partials[m].at[0], inb.at[m], in_sem.at[m]) for m in range(2)]
    for copy in loads:
        copy.start()
    barrier = pltpu.get_barrier_semaphore()
    greeted = [*step_x, *step_y, sibling, *column]
    for peer in greeted:
        pl.semaphore_signal(barrier, 1, device_id=peer, device_id_type=MESH)
    pltpu.make_async_copy(rows_hbm, row_state, w_sem.at[0]).start()
    pltpu.make_async_copy(cols_hbm, col_state, w_sem.at[1]).start()

    def own_block(k, i, core):
        m, first, wide = CHUNKS[k]
        owner = (lax.rem(y + i // NX, NY) * NX + lax.rem(x + i % NX, NX)) * NC + core
        start = pl.multiple_of(owner * BLOCK + first, LANE)
        return inb[m, :, pl.ds(start, 2 * wide)].astype(jnp.float32)

    started = []

    def send(src, dst, send_sem, recv_sem, target):
        copy = pltpu.make_async_remote_copy(
            src_ref=src, dst_ref=dst, send_sem=send_sem, recv_sem=recv_sem, device_id=target, device_id_type=MESH
        )
        copy.start()
        started.append(copy)
        return copy

    def convert(k):
        wide = CHUNKS[k][2]

        def one(i, carry):
            ry, rx = i // NX, i % NX
            value = own_block(k, i, 1 - c)
            for h in range(2):
                part = value[:, h * wide : (h + 1) * wide]
                give[k][0, h, rx, ry] = part[:HALF]
                give[k][1, h, ry, rx] = part[HALF:]
            return carry

        lax.fori_loop(0, NY * NX, one, 0, unroll=4)

    def exchange(k):
        return send(give[k], work[k], core_send.at[k], core_recv.at[k], sibling)

    def add_own(k):
        wide = CHUNKS[k][2]

        def one(i, carry):
            ry, rx = i // NX, i % NX
            value = own_block(k, i, c)
            for h in range(2):
                part = value[:, h * wide : (h + 1) * wide]
                work[k][0, h, rx, ry] = work[k][0, h, rx, ry] + part[:HALF]
                work[k][1, h, ry, rx] = work[k][1, h, ry, rx] + part[HALF:]
            return carry

        lax.fori_loop(0, NY * NX, one, 0, unroll=4)

    near = (1, 3)
    pairs = [(p, h) for h in range(2) for p in range(2)]
    copies = {}

    def first_sends(k):
        for p, h in pairs:
            step = (step_x, step_y)[p]
            copies[k, p, h, "far"] = send(
                work[k].at[p, h, 2], far[k].at[p, h], s1_send.at[k, p, h, 0], s1_recv.at[k, p, h, 0], step[h])
        for p, h in pairs:
            step = (step_x, step_y)[p]
            copies[k, p, h, "direct"] = send(
                work[k].at[p, h, near[1 - h]], direct[k].at[p, h], s1_send.at[k, p, h, 1], s1_recv.at[k, p, h, 1],
                step[1 - h])

    def first_join(k):
        for p, h in pairs:
            step = (step_x, step_y)[p]
            copies[k, p, h, "far"].wait_recv()
            work[k][p, h, near[h]] = work[k][p, h, near[h]] + far[k][p, h]
            copies[k, p, h, "acc"] = send(
                work[k].at[p, h, near[h]], acc[k].at[p, h], s1_send.at[k, p, h, 2], s1_recv.at[k, p, h, 2], step[h])

    def second_sends(k):
        for p, h in pairs:
            step = (step_y, step_x)[p]
            copies[k, p, h, "direct"].wait_recv()
            copies[k, p, h, "acc"].wait_recv()
            work[k][p, h, 0] = work[k][p, h, 0] + direct[k][p, h] + acc[k][p, h]
            if k >= K - SHORT:
                opposite = (device(z, y + 2, x, c), device(z, y, x + 2, c))[p]
                copies[k, p, h, "far2"] = send(
                    work[k].at[p, h, 0, 2], far2[k].at[p, h], s2_send.at[k, p, h, 0], s2_recv.at[k, p, h, 0], opposite)
                copies[k, p, h, "acc2"] = send(
                    work[k].at[p, h, 0, near[h]], acc2[k].at[p, h], s2_send.at[k, p, h, 2], s2_recv.at[k, p, h, 2],
                    step[h])
                copies[k, p, h, "direct2"] = send(
                    work[k].at[p, h, 0, near[1 - h]], direct2[k].at[p, h], s2_send.at[k, p, h, 1],
                    s2_recv.at[k, p, h, 1], step[1 - h])
                continue
            copies[k, p, h, "far2"] = send(
                work[k].at[p, h, 0, 2], far2[k].at[p, h], s2_send.at[k, p, h, 0], s2_recv.at[k, p, h, 0], step[h])
            copies[k, p, h, "direct2"] = send(
                work[k].at[p, h, 0, near[1 - h]], direct2[k].at[p, h], s2_send.at[k, p, h, 1],
                s2_recv.at[k, p, h, 1], step[1 - h])

    def second_join(k):
        if k >= K - SHORT:
            return
        for p, h in pairs:
            step = (step_y, step_x)[p]
            copies[k, p, h, "far2"].wait_recv()
            work[k][p, h, 0, near[h]] = work[k][p, h, 0, near[h]] + far2[k][p, h]
            copies[k, p, h, "acc2"] = send(
                work[k].at[p, h, 0, near[h]], acc2[k].at[p, h], s2_send.at[k, p, h, 2], s2_recv.at[k, p, h, 2],
                step[h])

    lane_sums = [None, None]

    def lanes(value):
        total = value[:, :LANE]
        for j in range(1, value.shape[1] // LANE):
            total = total + value[:, j * LANE : (j + 1) * LANE]
        return total

    def finish(k):
        m, first, wide = CHUNKS[k]
        for p, h in pairs:
            copies[k, p, h, "direct2"].wait_recv()
            copies[k, p, h, "acc2"].wait_recv()
            total = work[k][p, h, 0, 0] + direct2[k][p, h] + acc2[k][p, h]
            if k >= K - SHORT:
                copies[k, p, h, "far2"].wait_recv()
                total = total + far2[k][p, h]
            grad[m, p * HALF : (p + 1) * HALF, first + h * wide : first + (h + 1) * wide] = total
        g = grad[m, :, first : first + 2 * wide]
        squares = g * g
        col_all[k][z] = jnp.sum(squares, axis=0, keepdims=True)
        for i, peer in enumerate(column):
            send(col_all[k].at[z], col_all[k].at[z], col_send.at[k, i], col_recv.at[k, i], peer)
        part = lanes(squares)
        lane_sums[m] = part if lane_sums[m] is None else lane_sums[m] + part

    def wait_columns(k):
        for i in range(NZ - 1):
            source = lax.rem(z + NZ - (4, 3, 5, 2, 6, 1, 7)[i], NZ)
            pltpu.make_async_remote_copy(
                src_ref=col_all[k].at[source], dst_ref=col_all[k].at[source], send_sem=col_send.at[k, i],
                recv_sem=col_recv.at[k, i], device_id=sibling, device_id_type=MESH).wait_recv()

    for k in range(K):
        if k == 0 or CHUNKS[k][0] != CHUNKS[k - 1][0]:
            loads[CHUNKS[k][0]].wait()
        convert(k)
        if k == 0:
            pl.semaphore_wait(barrier, len(greeted))
        copies[k, "core"] = exchange(k)
        if k > 0:
            copies[k - 1, "core"].wait_recv()
            add_own(k - 1)
            first_sends(k - 1)
    copies[K - 1, "core"].wait_recv()
    add_own(K - 1)
    first_sends(K - 1)
    for k in range(K):
        first_join(k)
    for k in range(K):
        second_sends(k)
    for k in range(K):
        second_join(k)
    for k in range(K):
        finish(k)

    row_id = lax.broadcasted_iota(jnp.int32, (16, LANE), 0)
    lane_id = lax.broadcasted_iota(jnp.int32, (16, LANE), 1)
    lane_one = lax.broadcasted_iota(jnp.int32, (1, LANE), 1)
    small_row = lax.broadcasted_iota(jnp.int32, (16, 16), 0)
    small_lane = lax.broadcasted_iota(jnp.int32, (16, 16), 1)

    row_sums = [jnp.sum(lane_sums[m], axis=1, keepdims=True) for m in range(2)]
    for i, ref in enumerate((row_state, col_state)):
        pltpu.make_async_copy(ref, ref, w_sem.at[i]).wait()
    old_rows = [
        jnp.sum(jnp.where(small_row == small_lane, row_state[m : m + 1, :], 0.0), axis=1, keepdims=True)
        for m in range(2)
    ]

    scaled = [None, None]
    for k in range(K):
        m, first, wide = CHUNKS[k]
        wait_columns(k)
        total = col_all[k][0]
        for j in range(1, NZ):
            total = total + col_all[k][j]
        span = slice(first, first + 2 * wide)
        fresh = DECAY * col_state[m : m + 1, span] + (1.0 - DECAY) * total / ROWS
        new_cols[m : m + 1, span] = fresh
        g = grad[m, :, span]
        part = lanes(g * g * (1.0 / fresh))
        scaled[m] = part if scaled[m] is None else scaled[m] + part
    scaled = [jnp.sum(scaled[m], axis=1, keepdims=True) for m in range(2)]

    packed = jnp.zeros((16, LANE), jnp.float32)
    for q, value in enumerate(row_sums + scaled):
        packed = jnp.where(lane_id == row_id + 16 * q, value, packed)
    row_all[d] = jnp.sum(packed, axis=0, keepdims=True)
    for i, peer in enumerate(plane):
        send(row_all.at[d], row_all.at[d], row_send.at[i], row_recv.at[i], peer)

    out_cols = pltpu.make_async_copy(new_cols, new_cols_hbm, out_sem.at[0])
    out_cols.start()
    for m in range(2):
        grad[m] = grad[m] * lax.rsqrt(new_cols[m : m + 1, :])

    offsets = [
        (dy, dx, dc) for dy in (2, 1, 3, 0) for dx in (2, 1, 3, 0) for dc in (1, 0) if (dy, dx, dc) != (0, 0, 0)
    ]
    for i, (dy, dx, dc) in enumerate(offsets):
        source = device(z, y + NY - dy, x + NX - dx, c + dc)[1]
        pltpu.make_async_remote_copy(
            src_ref=row_all.at[source], dst_ref=row_all.at[source], send_sem=row_send.at[i],
            recv_sem=row_recv.at[i], device_id=sibling, device_id_type=MESH).wait_recv()
    total = row_all[0]
    for j in range(1, NDP):
        total = total + row_all[j]
    spread = jnp.broadcast_to(total, (16, LANE))
    part = [
        jnp.sum(jnp.where(lane_id == row_id + 16 * q, spread, 0.0), axis=1, keepdims=True) for q in range(4)
    ]
    fresh_rows = [DECAY * old_rows[m] + (1.0 - DECAY) * part[m] / FF for m in range(2)]
    message = jnp.zeros((1, LANE), jnp.float32)
    for m in range(2):
        message = jnp.where(lane_one == m, jnp.sum(part[2 + m] / fresh_rows[m], axis=0, keepdims=True), message)
        message = jnp.where(lane_one == 2 + m, jnp.sum(fresh_rows[m], axis=0, keepdims=True), message)
    sum_all[z] = message
    for i, peer in enumerate(column):
        send(sum_all.at[z], sum_all.at[z], sum_send.at[i], sum_recv.at[i], peer)

    for m in range(2):
        new_rows[m : m + 1, :] = jnp.sum(
            jnp.where(small_row == small_lane, fresh_rows[m], 0.0), axis=0, keepdims=True)
        grad[m] = grad[m] * lax.rsqrt(fresh_rows[m])
    out_rows = pltpu.make_async_copy(new_rows, new_rows_hbm, out_sem.at[1])
    out_rows.start()
    out_shape = pltpu.make_async_copy(grad, shape_hbm, out_sem.at[2])
    out_shape.start()
    for copy in started[:-len(column)]:
        copy.wait_send()

    for i in range(NZ - 1):
        source = lax.rem(z + NZ - (4, 3, 5, 2, 6, 1, 7)[i], NZ)
        pltpu.make_async_remote_copy(
            src_ref=sum_all.at[source], dst_ref=sum_all.at[source], send_sem=sum_send.at[i],
            recv_sem=sum_recv.at[i], device_id=sibling, device_id_type=MESH).wait_recv()
    total = sum_all[0]
    for j in range(1, NZ):
        total = total + sum_all[j]
    sums[...] = total
    out_sums = pltpu.make_async_copy(sums, sums_hbm, out_sem.at[3])
    out_sums.start()
    for copy in started[-len(column):]:
        copy.wait_send()
    for out in (out_cols, out_rows, out_shape, out_sums):
        out.wait()


def apply(
    shape, sums, rows, cols, gate_w, up_w,
    new_gate_hbm, new_up_hbm, new_rows_hbm, new_cols_hbm,
    result, out_sem,
):
    outs = [
        pltpu.make_async_copy(rows, new_rows_hbm, out_sem.at[2]),
        pltpu.make_async_copy(cols, new_cols_hbm, out_sem.at[3]),
    ]
    for copy in outs:
        copy.start()
    lane = lax.broadcasted_iota(jnp.int32, (1, LANE), 1)
    total = sums[...]
    for m in range(2):
        squares = jnp.sum(jnp.where(lane == m, total, 0.0), axis=1, keepdims=True)
        mean = jnp.sum(jnp.where(lane == 2 + m, total, 0.0), axis=1, keepdims=True) / ROWS
        root = jnp.sqrt(mean)
        rms = root * jnp.sqrt(squares / (ROWS * FF))
        scale = STEP * root / jnp.maximum(1.0, rms)
        result[m] = (gate_w, up_w)[m][...] - shape[m] * scale
        out = pltpu.make_async_copy(result.at[m], (new_gate_hbm, new_up_hbm)[m], out_sem.at[m])
        out.start()
        outs.append(out)
    for out in outs:
        out.wait()


def on_device(gate_partials, up_partials, gate_weight, up_weight, row_state, col_state):
    f32 = jnp.float32
    dma = pltpu.SemaphoreType.DMA
    shape, sums, new_rows, new_cols = pl.pallas_call(
        kernel,
        out_shape=(
            jax.ShapeDtypeStruct((2, 16, BLOCK), f32),
            jax.ShapeDtypeStruct((1, LANE), f32),
            jax.ShapeDtypeStruct((2, 16), f32),
            jax.ShapeDtypeStruct((2, BLOCK), f32),
        ),
        in_specs=[pl.BlockSpec(memory_space=pltpu.HBM)] * 4,
        out_specs=(pl.BlockSpec(memory_space=pl.ANY),) * 4,
        scratch_shapes=[
            pltpu.VMEM((2, 16, FF), jnp.bfloat16),
            tuple(pltpu.VMEM((2, 2, 4, 4, HALF, wide), f32) for _, _, wide in CHUNKS),
            tuple(pltpu.VMEM((2, 2, 4, 4, HALF, wide), f32) for _, _, wide in CHUNKS),
            tuple(pltpu.VMEM((2, 2, 4, HALF, wide), f32) for _, _, wide in CHUNKS),
            tuple(pltpu.VMEM((2, 2, 4, HALF, wide), f32) for _, _, wide in CHUNKS),
            tuple(pltpu.VMEM((2, 2, 4, HALF, wide), f32) for _, _, wide in CHUNKS),
            tuple(pltpu.VMEM((2, 2, HALF, wide), f32) for _, _, wide in CHUNKS),
            tuple(pltpu.VMEM((2, 2, HALF, wide), f32) for _, _, wide in CHUNKS),
            tuple(pltpu.VMEM((2, 2, HALF, wide), f32) for _, _, wide in CHUNKS),
            pltpu.VMEM((2, 16, BLOCK), f32),
            pltpu.VMEM((2, 16), f32),
            pltpu.VMEM((2, BLOCK), f32),
            pltpu.VMEM((2, 16), f32),
            pltpu.VMEM((2, BLOCK), f32),
            tuple(pltpu.VMEM((NZ, 1, 2 * wide), f32) for _, _, wide in CHUNKS),
            pltpu.VMEM((NDP, 1, LANE), f32),
            pltpu.VMEM((NZ, 1, LANE), f32),
            pltpu.VMEM((1, LANE), f32),
            dma((2,)),
            dma((K,)),
            dma((K,)),
            dma((K, 2, 2, 3)),
            dma((K, 2, 2, 3)),
            dma((K, 2, 2, 3)),
            dma((K, 2, 2, 3)),
            dma((K, NZ - 1)),
            dma((K, NZ - 1)),
            dma((NDP - 1,)),
            dma((NDP - 1,)),
            dma((NZ - 1,)),
            dma((NZ - 1,)),
            dma((2,)),
            dma((4,)),
        ],
        compiler_params=pltpu.CompilerParams(
            collective_id=0, has_side_effects=True, vmem_limit_bytes=53 * 1024 * 1024
        ),
    )(gate_partials, up_partials, row_state, col_state)
    return pl.pallas_call(
        apply,
        out_shape=(
            jax.ShapeDtypeStruct((16, BLOCK), f32),
            jax.ShapeDtypeStruct((16, BLOCK), f32),
            jax.ShapeDtypeStruct((2, 16), f32),
            jax.ShapeDtypeStruct((2, BLOCK), f32),
        ),
        in_specs=[pl.BlockSpec(memory_space=pltpu.VMEM)] * 6,
        out_specs=(pl.BlockSpec(memory_space=pl.ANY),) * 4,
        scratch_shapes=[
            pltpu.VMEM((2, 16, BLOCK), f32),
            dma((4,)),
        ],
        compiler_params=pltpu.CompilerParams(vmem_limit_bytes=53 * 1024 * 1024),
    )(shape, sums, new_rows, new_cols, gate_weight, up_weight)


def solution(mesh):
    placed = (
        P("dp", "mp", None),
        P("dp", "mp", None),
        P("mp", "dp"),
        P("mp", "dp"),
        P(None, "mp"),
        P(None, "dp"),
    )
    return jax.shard_map(
        on_device,
        mesh=mesh,
        in_specs=placed,
        out_specs=(P("mp", "dp"), P("mp", "dp"), P(None, "mp"), P(None, "dp")),
        check_vma=False,
    )
```

```python
import functools

import jax
import jax.numpy as jnp
from jax import lax
from jax.experimental import pallas as pl
from jax.experimental.pallas import tpu as pltpu
from jax.sharding import PartitionSpec as P

ROWS = 128
FF = 73728
DECAY = 0.8
STEP = 0.5
NZ, NY, NX, NC = 8, 4, 4, 2
NDP = NY * NX * NC
BLOCK = FF // NDP
HALF = 8
LANE = 128
TILES = ((3, 6), (6, 3))
CHUNKS = tuple(
    (m, 2 * LANE * sum(TILES[m][:j]), LANE * n) for m in range(2) for j, n in enumerate(TILES[m])
)
K = len(CHUNKS)
MESH = pl.DeviceIdType.MESH


def kernel(
    gate_hbm, up_hbm, states_hbm,
    shape_hbm, sums_hbm, new_rows_hbm, new_cols_hbm,
    inb, give, work, far, acc, direct, far2, acc2, direct2, grad,
    states, new_rows, new_cols, col_all, row_all, sum_all, sums,
    in_sem, core_send, core_recv, s1_send, s1_recv, s2_send, s2_recv,
    col_send, col_recv, row_send, row_recv, sum_send, sum_recv, w_sem, out_sem,
):
    z = lax.axis_index("mp")
    d = lax.axis_index("dp")
    y, x, c = d // (NX * NC), (d // NC) % NX, d % NC

    def device(zz, yy, xx, cc):
        return (lax.rem(zz, NZ), (lax.rem(yy, NY) * NX + lax.rem(xx, NX)) * NC + lax.rem(cc, NC))

    sibling = device(z, y, x, c + 1)
    step_x = (device(z, y, x + 1, c), device(z, y, x + NX - 1, c))
    step_y = (device(z, y + 1, x, c), device(z, y + NY - 1, x, c))
    plane = [
        device(z, y + dy, x + dx, c + dc)
        for dy in (2, 1, 3, 0) for dx in (2, 1, 3, 0) for dc in (1, 0) if (dy, dx, dc) != (0, 0, 0)
    ]
    column = [device(z + k, y, x, c) for k in (4, 3, 5, 2, 6, 1, 7)]

    partials = (gate_hbm, up_hbm)

    loads = [pltpu.make_async_copy(partials[m].at[0], inb.at[m], in_sem.at[m]) for m in range(2)]
    for copy in loads:
        copy.start()
    barrier = pltpu.get_barrier_semaphore()
    greeted = [*step_x, *step_y, sibling, *column]
    for peer in greeted:
        pl.semaphore_signal(barrier, 1, device_id=peer, device_id_type=MESH)
    pltpu.make_async_copy(states_hbm, states, w_sem.at[0]).start()

    def own_block(k, i, core):
        m, first, wide = CHUNKS[k]
        owner = (lax.rem(y + i // NX, NY) * NX + lax.rem(x + i % NX, NX)) * NC + core
        start = pl.multiple_of(owner * BLOCK + first, LANE)
        return inb[m, :, pl.ds(start, 2 * wide)].astype(jnp.float32)

    started = []

    def send(src, dst, send_sem, recv_sem, target):
        copy = pltpu.make_async_remote_copy(
            src_ref=src, dst_ref=dst, send_sem=send_sem, recv_sem=recv_sem, device_id=target, device_id_type=MESH
        )
        copy.start()
        started.append(copy)
        return copy

    def convert(k):
        wide = CHUNKS[k][2]

        def one(i, carry):
            ry, rx = i // NX, i % NX
            value = own_block(k, i, 1 - c)
            for h in range(2):
                part = value[:, h * wide : (h + 1) * wide]
                give[k][0, h, rx, ry] = part[:HALF]
                give[k][1, h, ry, rx] = part[HALF:]
            return carry

        lax.fori_loop(0, NY * NX, one, 0, unroll=16)

    def exchange(k):
        return send(give[k], work[k], core_send.at[k], core_recv.at[k], sibling)

    def add_own(k):
        wide = CHUNKS[k][2]

        def one(i, carry):
            ry, rx = i // NX, i % NX
            value = own_block(k, i, c)
            for h in range(2):
                part = value[:, h * wide : (h + 1) * wide]
                work[k][0, h, rx, ry] = work[k][0, h, rx, ry] + part[:HALF]
                work[k][1, h, ry, rx] = work[k][1, h, ry, rx] + part[HALF:]
            return carry

        lax.fori_loop(0, NY * NX, one, 0, unroll=16)

    near = (1, 3)
    pairs = [(p, h) for h in range(2) for p in range(2)]
    copies = {}

    def first_sends(k):
        for p, h in pairs:
            step = (step_x, step_y)[p]
            copies[k, p, h, "far"] = send(
                work[k].at[p, h, 2], far[k].at[p, h], s1_send.at[k, p, h, 0], s1_recv.at[k, p, h, 0], step[h])
        for p, h in pairs:
            step = (step_x, step_y)[p]
            copies[k, p, h, "direct"] = send(
                work[k].at[p, h, near[1 - h]], direct[k].at[p, h], s1_send.at[k, p, h, 1], s1_recv.at[k, p, h, 1],
                step[1 - h])

    def first_join(k):
        for p, h in pairs:
            step = (step_x, step_y)[p]
            copies[k, p, h, "far"].wait_recv()
            work[k][p, h, near[h]] = work[k][p, h, near[h]] + far[k][p, h]
            copies[k, p, h, "acc"] = send(
                work[k].at[p, h, near[h]], acc[k].at[p, h], s1_send.at[k, p, h, 2], s1_recv.at[k, p, h, 2], step[h])

    def second_sends(k):
        for p, h in pairs:
            step = (step_y, step_x)[p]
            copies[k, p, h, "direct"].wait_recv()
            copies[k, p, h, "acc"].wait_recv()
            work[k][p, h, 0] = work[k][p, h, 0] + direct[k][p, h] + acc[k][p, h]
            copies[k, p, h, "far2"] = send(
                work[k].at[p, h, 0, 2], far2[k].at[p, h], s2_send.at[k, p, h, 0], s2_recv.at[k, p, h, 0], step[h])
            copies[k, p, h, "direct2"] = send(
                work[k].at[p, h, 0, near[1 - h]], direct2[k].at[p, h], s2_send.at[k, p, h, 1],
                s2_recv.at[k, p, h, 1], step[1 - h])

    def second_join(k):
        for p, h in pairs:
            step = (step_y, step_x)[p]
            copies[k, p, h, "far2"].wait_recv()
            work[k][p, h, 0, near[h]] = work[k][p, h, 0, near[h]] + far2[k][p, h]
            copies[k, p, h, "acc2"] = send(
                work[k].at[p, h, 0, near[h]], acc2[k].at[p, h], s2_send.at[k, p, h, 2], s2_recv.at[k, p, h, 2],
                step[h])

    lane_sums = [None, None]

    def lanes(value):
        total = value[:, :LANE]
        for j in range(1, value.shape[1] // LANE):
            total = total + value[:, j * LANE : (j + 1) * LANE]
        return total

    def finish(k):
        m, first, wide = CHUNKS[k]
        for p, h in pairs:
            copies[k, p, h, "direct2"].wait_recv()
            copies[k, p, h, "acc2"].wait_recv()
            total = work[k][p, h, 0, 0] + direct2[k][p, h] + acc2[k][p, h]
            grad[m, p * HALF : (p + 1) * HALF, first + h * wide : first + (h + 1) * wide] = total
        g = grad[m, :, first : first + 2 * wide]
        squares = g * g
        col_all[k][z] = jnp.sum(squares, axis=0, keepdims=True)
        for i, peer in enumerate(column):
            send(col_all[k].at[z], col_all[k].at[z], col_send.at[k, i], col_recv.at[k, i], peer)
        part = lanes(squares)
        lane_sums[m] = part if lane_sums[m] is None else lane_sums[m] + part

    def wait_columns(k):
        for i in range(NZ - 1):
            source = lax.rem(z + NZ - (4, 3, 5, 2, 6, 1, 7)[i], NZ)
            pltpu.make_async_remote_copy(
                src_ref=col_all[k].at[source], dst_ref=col_all[k].at[source], send_sem=col_send.at[k, i],
                recv_sem=col_recv.at[k, i], device_id=sibling, device_id_type=MESH).wait_recv()

    for k in range(K):
        if k == 0 or CHUNKS[k][0] != CHUNKS[k - 1][0]:
            loads[CHUNKS[k][0]].wait()
        convert(k)
        if k == 0:
            pl.semaphore_wait(barrier, len(greeted))
        copies[k, "core"] = exchange(k)
        if k > 0:
            copies[k - 1, "core"].wait_recv()
            add_own(k - 1)
            first_sends(k - 1)
    copies[K - 1, "core"].wait_recv()
    add_own(K - 1)
    first_sends(K - 1)
    for k in range(K):
        first_join(k)
    for k in range(K):
        second_sends(k)
    for k in range(K):
        second_join(k)
    for k in range(K):
        finish(k)

    row_id = lax.broadcasted_iota(jnp.int32, (16, LANE), 0)
    lane_id = lax.broadcasted_iota(jnp.int32, (16, LANE), 1)
    lane_one = lax.broadcasted_iota(jnp.int32, (1, LANE), 1)
    small_row = lax.broadcasted_iota(jnp.int32, (16, 16), 0)
    small_lane = lax.broadcasted_iota(jnp.int32, (16, 16), 1)

    row_sums = [jnp.sum(lane_sums[m], axis=1, keepdims=True) for m in range(2)]
    pltpu.make_async_copy(states, states, w_sem.at[0]).wait()
    old_rows = [
        jnp.sum(jnp.where(small_row == small_lane, states[m : m + 1, BLOCK:], 0.0), axis=1, keepdims=True)
        for m in range(2)
    ]

    scaled = [None, None]
    for k in range(K):
        m, first, wide = CHUNKS[k]
        wait_columns(k)
        total = col_all[k][0]
        for j in range(1, NZ):
            total = total + col_all[k][j]
        span = slice(first, first + 2 * wide)
        fresh = DECAY * states[m : m + 1, span] + (1.0 - DECAY) * total / ROWS
        new_cols[m : m + 1, span] = fresh
        g = grad[m, :, span]
        part = lanes(g * g * (1.0 / fresh))
        scaled[m] = part if scaled[m] is None else scaled[m] + part
    scaled = [jnp.sum(scaled[m], axis=1, keepdims=True) for m in range(2)]

    packed = jnp.zeros((16, LANE), jnp.float32)
    for q, value in enumerate(row_sums + scaled):
        packed = jnp.where(lane_id == row_id + 16 * q, value, packed)
    row_all[d] = jnp.sum(packed, axis=0, keepdims=True)
    for i, peer in enumerate(plane):
        send(row_all.at[d], row_all.at[d], row_send.at[i], row_recv.at[i], peer)

    out_cols = pltpu.make_async_copy(new_cols, new_cols_hbm, out_sem.at[0])
    out_cols.start()
    for m in range(2):
        grad[m] = grad[m] * lax.rsqrt(new_cols[m : m + 1, :])

    offsets = [
        (dy, dx, dc) for dy in (2, 1, 3, 0) for dx in (2, 1, 3, 0) for dc in (1, 0) if (dy, dx, dc) != (0, 0, 0)
    ]
    for i, (dy, dx, dc) in enumerate(offsets):
        source = device(z, y + NY - dy, x + NX - dx, c + dc)[1]
        pltpu.make_async_remote_copy(
            src_ref=row_all.at[source], dst_ref=row_all.at[source], send_sem=row_send.at[i],
            recv_sem=row_recv.at[i], device_id=sibling, device_id_type=MESH).wait_recv()
    total = row_all[0]
    for j in range(1, NDP):
        total = total + row_all[j]
    spread = jnp.broadcast_to(total, (16, LANE))
    part = [
        jnp.sum(jnp.where(lane_id == row_id + 16 * q, spread, 0.0), axis=1, keepdims=True) for q in range(4)
    ]
    fresh_rows = [DECAY * old_rows[m] + (1.0 - DECAY) * part[m] / FF for m in range(2)]
    message = jnp.zeros((1, LANE), jnp.float32)
    for m in range(2):
        message = jnp.where(lane_one == m, jnp.sum(part[2 + m] / fresh_rows[m], axis=0, keepdims=True), message)
        message = jnp.where(lane_one == 2 + m, jnp.sum(fresh_rows[m], axis=0, keepdims=True), message)
    sum_all[z] = message
    for i, peer in enumerate(column):
        send(sum_all.at[z], sum_all.at[z], sum_send.at[i], sum_recv.at[i], peer)

    for m in range(2):
        new_rows[m : m + 1, :] = jnp.sum(
            jnp.where(small_row == small_lane, fresh_rows[m], 0.0), axis=0, keepdims=True)
        grad[m] = grad[m] * lax.rsqrt(fresh_rows[m])
    out_rows = pltpu.make_async_copy(new_rows, new_rows_hbm, out_sem.at[1])
    out_rows.start()
    out_shape = pltpu.make_async_copy(grad, shape_hbm, out_sem.at[2])
    out_shape.start()
    for copy in started[:-len(column)]:
        copy.wait_send()

    for i in range(NZ - 1):
        source = lax.rem(z + NZ - (4, 3, 5, 2, 6, 1, 7)[i], NZ)
        pltpu.make_async_remote_copy(
            src_ref=sum_all.at[source], dst_ref=sum_all.at[source], send_sem=sum_send.at[i],
            recv_sem=sum_recv.at[i], device_id=sibling, device_id_type=MESH).wait_recv()
    total = sum_all[0]
    for j in range(1, NZ):
        total = total + sum_all[j]
    sums[...] = total
    out_sums = pltpu.make_async_copy(sums, sums_hbm, out_sem.at[3])
    out_sums.start()
    for copy in started[-len(column):]:
        copy.wait_send()
    for out in (out_cols, out_rows, out_shape, out_sums):
        out.wait()


def apply(
    shape, sums, rows, cols, gate_w, up_w,
    new_gate_hbm, new_up_hbm, new_rows_hbm, new_cols_hbm,
    result, out_sem,
):
    outs = [
        pltpu.make_async_copy(rows, new_rows_hbm, out_sem.at[2]),
        pltpu.make_async_copy(cols, new_cols_hbm, out_sem.at[3]),
    ]
    for copy in outs:
        copy.start()
    lane = lax.broadcasted_iota(jnp.int32, (1, LANE), 1)
    total = sums[...]
    for m in range(2):
        squares = jnp.sum(jnp.where(lane == m, total, 0.0), axis=1, keepdims=True)
        mean = jnp.sum(jnp.where(lane == 2 + m, total, 0.0), axis=1, keepdims=True) / ROWS
        root = jnp.sqrt(mean)
        rms = root * jnp.sqrt(squares / (ROWS * FF))
        scale = STEP * root / jnp.maximum(1.0, rms)
        result[m] = (gate_w, up_w)[m][...] - shape[m] * scale
        out = pltpu.make_async_copy(result.at[m], (new_gate_hbm, new_up_hbm)[m], out_sem.at[m])
        out.start()
        outs.append(out)
    for out in outs:
        out.wait()


def on_device(gate_partials, up_partials, gate_weight, up_weight, row_state, col_state):
    f32 = jnp.float32
    dma = pltpu.SemaphoreType.DMA
    shape, sums, new_rows, new_cols = pl.pallas_call(
        kernel,
        out_shape=(
            jax.ShapeDtypeStruct((2, 16, BLOCK), f32),
            jax.ShapeDtypeStruct((1, LANE), f32),
            jax.ShapeDtypeStruct((2, 16), f32),
            jax.ShapeDtypeStruct((2, BLOCK), f32),
        ),
        in_specs=[pl.BlockSpec(memory_space=pltpu.HBM)] * 3,
        out_specs=(pl.BlockSpec(memory_space=pl.ANY),) * 4,
        scratch_shapes=[
            pltpu.VMEM((2, 16, FF), jnp.bfloat16),
            tuple(pltpu.VMEM((2, 2, 4, 4, HALF, wide), f32) for _, _, wide in CHUNKS),
            tuple(pltpu.VMEM((2, 2, 4, 4, HALF, wide), f32) for _, _, wide in CHUNKS),
            tuple(pltpu.VMEM((2, 2, 4, HALF, wide), f32) for _, _, wide in CHUNKS),
            tuple(pltpu.VMEM((2, 2, 4, HALF, wide), f32) for _, _, wide in CHUNKS),
            tuple(pltpu.VMEM((2, 2, 4, HALF, wide), f32) for _, _, wide in CHUNKS),
            tuple(pltpu.VMEM((2, 2, HALF, wide), f32) for _, _, wide in CHUNKS),
            tuple(pltpu.VMEM((2, 2, HALF, wide), f32) for _, _, wide in CHUNKS),
            tuple(pltpu.VMEM((2, 2, HALF, wide), f32) for _, _, wide in CHUNKS),
            pltpu.VMEM((2, 16, BLOCK), f32),
            pltpu.VMEM((2, BLOCK + 16), f32),
            pltpu.VMEM((2, 16), f32),
            pltpu.VMEM((2, BLOCK), f32),
            tuple(pltpu.VMEM((NZ, 1, 2 * wide), f32) for _, _, wide in CHUNKS),
            pltpu.VMEM((NDP, 1, LANE), f32),
            pltpu.VMEM((NZ, 1, LANE), f32),
            pltpu.VMEM((1, LANE), f32),
            dma((2,)),
            dma((K,)),
            dma((K,)),
            dma((K, 2, 2, 3)),
            dma((K, 2, 2, 3)),
            dma((K, 2, 2, 3)),
            dma((K, 2, 2, 3)),
            dma((K, NZ - 1)),
            dma((K, NZ - 1)),
            dma((NDP - 1,)),
            dma((NDP - 1,)),
            dma((NZ - 1,)),
            dma((NZ - 1,)),
            dma((1,)),
            dma((4,)),
        ],
        compiler_params=pltpu.CompilerParams(
            collective_id=0, has_side_effects=True, vmem_limit_bytes=53 * 1024 * 1024
        ),
    )(gate_partials, up_partials, jnp.concatenate([col_state, row_state], axis=1))
    return pl.pallas_call(
        apply,
        out_shape=(
            jax.ShapeDtypeStruct((16, BLOCK), f32),
            jax.ShapeDtypeStruct((16, BLOCK), f32),
            jax.ShapeDtypeStruct((2, 16), f32),
            jax.ShapeDtypeStruct((2, BLOCK), f32),
        ),
        in_specs=[pl.BlockSpec(memory_space=pltpu.VMEM)] * 6,
        out_specs=(pl.BlockSpec(memory_space=pl.ANY),) * 4,
        scratch_shapes=[
            pltpu.VMEM((2, 16, BLOCK), f32),
            dma((4,)),
        ],
        compiler_params=pltpu.CompilerParams(vmem_limit_bytes=53 * 1024 * 1024),
    )(shape, sums, new_rows, new_cols, gate_weight, up_weight)


def solution(mesh):
    placed = (
        P("dp", "mp", None),
        P("dp", "mp", None),
        P("mp", "dp"),
        P("mp", "dp"),
        P(None, "mp"),
        P(None, "dp"),
    )
    return jax.shard_map(
        on_device,
        mesh=mesh,
        in_specs=placed,
        out_specs=(P("mp", "dp"), P("mp", "dp"), P(None, "mp"), P(None, "dp")),
        check_vma=False,
    )
```

```python
import functools

import jax
import jax.numpy as jnp
from jax import lax
from jax.experimental import pallas as pl
from jax.experimental.pallas import tpu as pltpu
from jax.sharding import PartitionSpec as P

ROWS = 128
FF = 73728
DECAY = 0.8
STEP = 0.5
NZ, NY, NX, NC = 8, 4, 4, 2
NDP = NY * NX * NC
BLOCK = FF // NDP
HALF = 8
LANE = 128
TILES = ((3, 6), (6, 3))
CHUNKS = tuple(
    (m, 2 * LANE * sum(TILES[m][:j]), LANE * n) for m in range(2) for j, n in enumerate(TILES[m])
)
K = len(CHUNKS)
MESH = pl.DeviceIdType.MESH


def kernel(
    gate_hbm, up_hbm, states_hbm,
    shape_hbm, sums_hbm, new_rows_hbm, new_cols_hbm,
    inb, give, work, far, acc, direct, far2, acc2, direct2, grad,
    states, new_rows, new_cols, col_all, row_all, sum_all, sums,
    in_sem, core_send, core_recv, s1_send, s1_recv, s2_send, s2_recv,
    col_send, col_recv, row_send, row_recv, sum_send, sum_recv, w_sem, out_sem,
):
    z = lax.axis_index("mp")
    d = lax.axis_index("dp")
    y, x, c = d // (NX * NC), (d // NC) % NX, d % NC

    def device(zz, yy, xx, cc):
        return (lax.rem(zz, NZ), (lax.rem(yy, NY) * NX + lax.rem(xx, NX)) * NC + lax.rem(cc, NC))

    sibling = device(z, y, x, c + 1)
    step_x = (device(z, y, x + 1, c), device(z, y, x + NX - 1, c))
    step_y = (device(z, y + 1, x, c), device(z, y + NY - 1, x, c))
    plane = [
        device(z, y + dy, x + dx, c + dc)
        for dy in (2, 1, 3, 0) for dx in (2, 1, 3, 0) for dc in (1, 0) if (dy, dx, dc) != (0, 0, 0)
    ]
    column = [device(z + k, y, x, c) for k in (4, 3, 5, 2, 6, 1, 7)]

    partials = (gate_hbm, up_hbm)

    loads = [pltpu.make_async_copy(partials[m].at[0], inb.at[m], in_sem.at[m]) for m in range(2)]
    for copy in loads:
        copy.start()
    barrier = pltpu.get_barrier_semaphore()
    greeted = [*step_x, *step_y, sibling, *column]
    for peer in greeted:
        pl.semaphore_signal(barrier, 1, device_id=peer, device_id_type=MESH)
    pltpu.make_async_copy(states_hbm, states, w_sem.at[0]).start()

    def own_block(k, i, core):
        m, first, wide = CHUNKS[k]
        owner = (lax.rem(y + i // NX, NY) * NX + lax.rem(x + i % NX, NX)) * NC + core
        start = pl.multiple_of(owner * BLOCK + first, LANE)
        return inb[m, :, pl.ds(start, 2 * wide)].astype(jnp.float32)

    started = []

    def send(src, dst, send_sem, recv_sem, target):
        copy = pltpu.make_async_remote_copy(
            src_ref=src, dst_ref=dst, send_sem=send_sem, recv_sem=recv_sem, device_id=target, device_id_type=MESH
        )
        copy.start()
        started.append(copy)
        return copy

    def convert(k):
        wide = CHUNKS[k][2]

        def one(i, carry):
            ry, rx = i // NX, i % NX
            value = own_block(k, i, 1 - c)
            for h in range(2):
                part = value[:, h * wide : (h + 1) * wide]
                give[k][0, h, rx, ry] = part[:HALF]
                give[k][1, h, ry, rx] = part[HALF:]
            return carry

        lax.fori_loop(0, NY * NX, one, 0, unroll=16)

    def exchange(k):
        return send(give[k], work[k], core_send.at[k], core_recv.at[k], sibling)

    every = [(ry, rx) for ry in range(NY) for rx in range(NX)]
    far_first = [q for q in every if 2 in q]
    others = [q for q in every if 2 not in q]

    def add_own(k, blocks):
        wide = CHUNKS[k][2]
        for ry, rx in blocks:
            value = own_block(k, ry * NX + rx, c)
            for h in range(2):
                part = value[:, h * wide : (h + 1) * wide]
                work[k][0, h, rx, ry] = work[k][0, h, rx, ry] + part[:HALF]
                work[k][1, h, ry, rx] = work[k][1, h, ry, rx] + part[HALF:]

    near = (1, 3)
    pairs = [(p, h) for h in range(2) for p in range(2)]
    copies = {}

    def first_sends(k):
        for p, h in pairs:
            step = (step_x, step_y)[p]
            copies[k, p, h, "far"] = send(
                work[k].at[p, h, 2], far[k].at[p, h], s1_send.at[k, p, h, 0], s1_recv.at[k, p, h, 0], step[h])
        add_own(k, others)
        for p, h in pairs:
            step = (step_x, step_y)[p]
            copies[k, p, h, "direct"] = send(
                work[k].at[p, h, near[1 - h]], direct[k].at[p, h], s1_send.at[k, p, h, 1], s1_recv.at[k, p, h, 1],
                step[1 - h])

    def first_join(k):
        for p, h in pairs:
            step = (step_x, step_y)[p]
            copies[k, p, h, "far"].wait_recv()
            work[k][p, h, near[h]] = work[k][p, h, near[h]] + far[k][p, h]
            copies[k, p, h, "acc"] = send(
                work[k].at[p, h, near[h]], acc[k].at[p, h], s1_send.at[k, p, h, 2], s1_recv.at[k, p, h, 2], step[h])

    def second_sends(k):
        for p, h in pairs:
            step = (step_y, step_x)[p]
            copies[k, p, h, "direct"].wait_recv()
            copies[k, p, h, "acc"].wait_recv()
            work[k][p, h, 0] = work[k][p, h, 0] + direct[k][p, h] + acc[k][p, h]
            copies[k, p, h, "far2"] = send(
                work[k].at[p, h, 0, 2], far2[k].at[p, h], s2_send.at[k, p, h, 0], s2_recv.at[k, p, h, 0], step[h])
            copies[k, p, h, "direct2"] = send(
                work[k].at[p, h, 0, near[1 - h]], direct2[k].at[p, h], s2_send.at[k, p, h, 1],
                s2_recv.at[k, p, h, 1], step[1 - h])

    def second_join(k):
        for p, h in pairs:
            step = (step_y, step_x)[p]
            copies[k, p, h, "far2"].wait_recv()
            work[k][p, h, 0, near[h]] = work[k][p, h, 0, near[h]] + far2[k][p, h]
            copies[k, p, h, "acc2"] = send(
                work[k].at[p, h, 0, near[h]], acc2[k].at[p, h], s2_send.at[k, p, h, 2], s2_recv.at[k, p, h, 2],
                step[h])

    lane_sums = [None, None]

    def lanes(value):
        total = value[:, :LANE]
        for j in range(1, value.shape[1] // LANE):
            total = total + value[:, j * LANE : (j + 1) * LANE]
        return total

    def finish(k):
        m, first, wide = CHUNKS[k]
        for p, h in pairs:
            copies[k, p, h, "direct2"].wait_recv()
            copies[k, p, h, "acc2"].wait_recv()
            total = work[k][p, h, 0, 0] + direct2[k][p, h] + acc2[k][p, h]
            grad[m, p * HALF : (p + 1) * HALF, first + h * wide : first + (h + 1) * wide] = total
        g = grad[m, :, first : first + 2 * wide]
        squares = g * g
        col_all[k][z] = jnp.sum(squares, axis=0, keepdims=True)
        for i, peer in enumerate(column):
            send(col_all[k].at[z], col_all[k].at[z], col_send.at[k, i], col_recv.at[k, i], peer)
        part = lanes(squares)
        lane_sums[m] = part if lane_sums[m] is None else lane_sums[m] + part

    def wait_columns(k):
        for i in range(NZ - 1):
            source = lax.rem(z + NZ - (4, 3, 5, 2, 6, 1, 7)[i], NZ)
            pltpu.make_async_remote_copy(
                src_ref=col_all[k].at[source], dst_ref=col_all[k].at[source], send_sem=col_send.at[k, i],
                recv_sem=col_recv.at[k, i], device_id=sibling, device_id_type=MESH).wait_recv()

    for k in range(K):
        if k == 0 or CHUNKS[k][0] != CHUNKS[k - 1][0]:
            loads[CHUNKS[k][0]].wait()
        convert(k)
        if k == 0:
            pl.semaphore_wait(barrier, len(greeted))
        copies[k, "core"] = exchange(k)
        if k > 0:
            copies[k - 1, "core"].wait_recv()
            add_own(k - 1, far_first)
            first_sends(k - 1)
    copies[K - 1, "core"].wait_recv()
    add_own(K - 1, far_first)
    first_sends(K - 1)
    for k in range(K):
        first_join(k)
    for k in range(K):
        second_sends(k)
    for k in range(K):
        second_join(k)
    for k in range(K):
        finish(k)

    row_id = lax.broadcasted_iota(jnp.int32, (16, LANE), 0)
    lane_id = lax.broadcasted_iota(jnp.int32, (16, LANE), 1)
    lane_one = lax.broadcasted_iota(jnp.int32, (1, LANE), 1)
    small_row = lax.broadcasted_iota(jnp.int32, (16, 16), 0)
    small_lane = lax.broadcasted_iota(jnp.int32, (16, 16), 1)

    row_sums = [jnp.sum(lane_sums[m], axis=1, keepdims=True) for m in range(2)]
    pltpu.make_async_copy(states, states, w_sem.at[0]).wait()
    old_rows = [
        jnp.sum(jnp.where(small_row == small_lane, states[m : m + 1, BLOCK:], 0.0), axis=1, keepdims=True)
        for m in range(2)
    ]

    scaled = [None, None]
    for k in range(K):
        m, first, wide = CHUNKS[k]
        wait_columns(k)
        total = col_all[k][0]
        for j in range(1, NZ):
            total = total + col_all[k][j]
        span = slice(first, first + 2 * wide)
        fresh = DECAY * states[m : m + 1, span] + (1.0 - DECAY) * total / ROWS
        new_cols[m : m + 1, span] = fresh
        g = grad[m, :, span]
        part = lanes(g * g * (1.0 / fresh))
        scaled[m] = part if scaled[m] is None else scaled[m] + part
    scaled = [jnp.sum(scaled[m], axis=1, keepdims=True) for m in range(2)]

    packed = jnp.zeros((16, LANE), jnp.float32)
    for q, value in enumerate(row_sums + scaled):
        packed = jnp.where(lane_id == row_id + 16 * q, value, packed)
    row_all[d] = jnp.sum(packed, axis=0, keepdims=True)
    for i, peer in enumerate(plane):
        send(row_all.at[d], row_all.at[d], row_send.at[i], row_recv.at[i], peer)

    out_cols = pltpu.make_async_copy(new_cols, new_cols_hbm, out_sem.at[0])
    out_cols.start()
    for m in range(2):
        grad[m] = grad[m] * lax.rsqrt(new_cols[m : m + 1, :])

    offsets = [
        (dy, dx, dc) for dy in (2, 1, 3, 0) for dx in (2, 1, 3, 0) for dc in (1, 0) if (dy, dx, dc) != (0, 0, 0)
    ]
    for i, (dy, dx, dc) in enumerate(offsets):
        source = device(z, y + NY - dy, x + NX - dx, c + dc)[1]
        pltpu.make_async_remote_copy(
            src_ref=row_all.at[source], dst_ref=row_all.at[source], send_sem=row_send.at[i],
            recv_sem=row_recv.at[i], device_id=sibling, device_id_type=MESH).wait_recv()
    total = row_all[0]
    for j in range(1, NDP):
        total = total + row_all[j]
    spread = jnp.broadcast_to(total, (16, LANE))
    part = [
        jnp.sum(jnp.where(lane_id == row_id + 16 * q, spread, 0.0), axis=1, keepdims=True) for q in range(4)
    ]
    fresh_rows = [DECAY * old_rows[m] + (1.0 - DECAY) * part[m] / FF for m in range(2)]
    message = jnp.zeros((1, LANE), jnp.float32)
    for m in range(2):
        message = jnp.where(lane_one == m, jnp.sum(part[2 + m] / fresh_rows[m], axis=0, keepdims=True), message)
        message = jnp.where(lane_one == 2 + m, jnp.sum(fresh_rows[m], axis=0, keepdims=True), message)
    sum_all[z] = message
    for i, peer in enumerate(column):
        send(sum_all.at[z], sum_all.at[z], sum_send.at[i], sum_recv.at[i], peer)

    for m in range(2):
        new_rows[m : m + 1, :] = jnp.sum(
            jnp.where(small_row == small_lane, fresh_rows[m], 0.0), axis=0, keepdims=True)
        grad[m] = grad[m] * lax.rsqrt(fresh_rows[m])
    out_rows = pltpu.make_async_copy(new_rows, new_rows_hbm, out_sem.at[1])
    out_rows.start()
    out_shape = pltpu.make_async_copy(grad, shape_hbm, out_sem.at[2])
    out_shape.start()
    for copy in started[:-len(column)]:
        copy.wait_send()

    for i in range(NZ - 1):
        source = lax.rem(z + NZ - (4, 3, 5, 2, 6, 1, 7)[i], NZ)
        pltpu.make_async_remote_copy(
            src_ref=sum_all.at[source], dst_ref=sum_all.at[source], send_sem=sum_send.at[i],
            recv_sem=sum_recv.at[i], device_id=sibling, device_id_type=MESH).wait_recv()
    total = sum_all[0]
    for j in range(1, NZ):
        total = total + sum_all[j]
    sums[...] = total
    out_sums = pltpu.make_async_copy(sums, sums_hbm, out_sem.at[3])
    out_sums.start()
    for copy in started[-len(column):]:
        copy.wait_send()
    for out in (out_cols, out_rows, out_shape, out_sums):
        out.wait()


def apply(
    shape, sums, rows, cols, gate_w, up_w,
    new_gate_hbm, new_up_hbm, new_rows_hbm, new_cols_hbm,
    result, out_sem,
):
    outs = [
        pltpu.make_async_copy(rows, new_rows_hbm, out_sem.at[2]),
        pltpu.make_async_copy(cols, new_cols_hbm, out_sem.at[3]),
    ]
    for copy in outs:
        copy.start()
    lane = lax.broadcasted_iota(jnp.int32, (1, LANE), 1)
    total = sums[...]
    for m in range(2):
        squares = jnp.sum(jnp.where(lane == m, total, 0.0), axis=1, keepdims=True)
        mean = jnp.sum(jnp.where(lane == 2 + m, total, 0.0), axis=1, keepdims=True) / ROWS
        root = jnp.sqrt(mean)
        rms = root * jnp.sqrt(squares / (ROWS * FF))
        scale = STEP * root / jnp.maximum(1.0, rms)
        result[m] = (gate_w, up_w)[m][...] - shape[m] * scale
        out = pltpu.make_async_copy(result.at[m], (new_gate_hbm, new_up_hbm)[m], out_sem.at[m])
        out.start()
        outs.append(out)
    for out in outs:
        out.wait()


def on_device(gate_partials, up_partials, gate_weight, up_weight, row_state, col_state):
    f32 = jnp.float32
    dma = pltpu.SemaphoreType.DMA
    shape, sums, new_rows, new_cols = pl.pallas_call(
        kernel,
        out_shape=(
            jax.ShapeDtypeStruct((2, 16, BLOCK), f32),
            jax.ShapeDtypeStruct((1, LANE), f32),
            jax.ShapeDtypeStruct((2, 16), f32),
            jax.ShapeDtypeStruct((2, BLOCK), f32),
        ),
        in_specs=[pl.BlockSpec(memory_space=pltpu.HBM)] * 3,
        out_specs=(pl.BlockSpec(memory_space=pl.ANY),) * 4,
        scratch_shapes=[
            pltpu.VMEM((2, 16, FF), jnp.bfloat16),
            tuple(pltpu.VMEM((2, 2, 4, 4, HALF, wide), f32) for _, _, wide in CHUNKS),
            tuple(pltpu.VMEM((2, 2, 4, 4, HALF, wide), f32) for _, _, wide in CHUNKS),
            tuple(pltpu.VMEM((2, 2, 4, HALF, wide), f32) for _, _, wide in CHUNKS),
            tuple(pltpu.VMEM((2, 2, 4, HALF, wide), f32) for _, _, wide in CHUNKS),
            tuple(pltpu.VMEM((2, 2, 4, HALF, wide), f32) for _, _, wide in CHUNKS),
            tuple(pltpu.VMEM((2, 2, HALF, wide), f32) for _, _, wide in CHUNKS),
            tuple(pltpu.VMEM((2, 2, HALF, wide), f32) for _, _, wide in CHUNKS),
            tuple(pltpu.VMEM((2, 2, HALF, wide), f32) for _, _, wide in CHUNKS),
            pltpu.VMEM((2, 16, BLOCK), f32),
            pltpu.VMEM((2, BLOCK + 16), f32),
            pltpu.VMEM((2, 16), f32),
            pltpu.VMEM((2, BLOCK), f32),
            tuple(pltpu.VMEM((NZ, 1, 2 * wide), f32) for _, _, wide in CHUNKS),
            pltpu.VMEM((NDP, 1, LANE), f32),
            pltpu.VMEM((NZ, 1, LANE), f32),
            pltpu.VMEM((1, LANE), f32),
            dma((2,)),
            dma((K,)),
            dma((K,)),
            dma((K, 2, 2, 3)),
            dma((K, 2, 2, 3)),
            dma((K, 2, 2, 3)),
            dma((K, 2, 2, 3)),
            dma((K, NZ - 1)),
            dma((K, NZ - 1)),
            dma((NDP - 1,)),
            dma((NDP - 1,)),
            dma((NZ - 1,)),
            dma((NZ - 1,)),
            dma((1,)),
            dma((4,)),
        ],
        compiler_params=pltpu.CompilerParams(
            collective_id=0, has_side_effects=True, vmem_limit_bytes=53 * 1024 * 1024
        ),
    )(gate_partials, up_partials, jnp.concatenate([col_state, row_state], axis=1))
    return pl.pallas_call(
        apply,
        out_shape=(
            jax.ShapeDtypeStruct((16, BLOCK), f32),
            jax.ShapeDtypeStruct((16, BLOCK), f32),
            jax.ShapeDtypeStruct((2, 16), f32),
            jax.ShapeDtypeStruct((2, BLOCK), f32),
        ),
        in_specs=[pl.BlockSpec(memory_space=pltpu.VMEM)] * 6,
        out_specs=(pl.BlockSpec(memory_space=pl.ANY),) * 4,
        scratch_shapes=[
            pltpu.VMEM((2, 16, BLOCK), f32),
            dma((4,)),
        ],
        compiler_params=pltpu.CompilerParams(vmem_limit_bytes=53 * 1024 * 1024),
    )(shape, sums, new_rows, new_cols, gate_weight, up_weight)


def solution(mesh):
    placed = (
        P("dp", "mp", None),
        P("dp", "mp", None),
        P("mp", "dp"),
        P("mp", "dp"),
        P(None, "mp"),
        P(None, "dp"),
    )
    return jax.shard_map(
        on_device,
        mesh=mesh,
        in_specs=placed,
        out_specs=(P("mp", "dp"), P("mp", "dp"), P(None, "mp"), P(None, "dp")),
        check_vma=False,
    )
```
